256 devices in a mesh: ctx: 64 (over z, y_lo, x), head: 4 (over y_hi, core).
Axes of the slice: x: 4, y: 4 (y_hi: 2, y_lo: 2; y = y_hi * 2 + y_lo), z: 8, core: 2. Of those that a mesh axis runs over, the one named last changes fastest.
Arguments:
- queries: bfloat16 [1536, 36864], P('ctx', 'head'), may hold values from -40 to 40
- kv_latent: bfloat16 [576, 8192], P(None, 'ctx'), may hold values from -6 to 6
- index_queries: bfloat16 [1536, 8192], P('ctx', 'head'), may hold values from -6 to 6
- index_keys: bfloat16 [8192, 128], P('ctx'), may hold values from -6 to 6
- head_weights: float32 [1536, 64], P('ctx', 'head'), may hold values from -600 to 600
- positions: int32 [1536], P('ctx'), may hold values from 0 to 8191, as said below
Outputs:
- grad_queries: float32 [1536, 8192], P('ctx', 'head')
- grad_keys: float32 [8192, 128], P(('ctx', 'head'))
The draws below stay inside these ranges and needn't reach their ends.
Inputs may be any that keep to these rules, and one draw needn't show every extreme that they name: Entries c * 24 to (c + 1) * 24 - 1 are positions among tokens c * 128 to (c + 1) * 128 - 1; the first entry of each such group is the first of those tokens and the second is the last.
All inputs are finite; a program needn't handle non-finite values.
Results may differ from the reference program's by a relative error of at most 0.013.
Values may be sent and summed in bfloat16 or wider, within the bound.
No kernel may reach another device: no remote copies, remote signals or barrier semaphores. Data moves between devices by JAX's collectives and lax.ppermute only.
A program may use at most 64 MiB of HBM per device.

```python
import math
import jax
import jax.numpy as jnp
from jax import lax

DL = 576
HEADS = 64
IHEADS = 64
DI = 128
TOK_DEV = 128
Q_DEV = 24
TOKENS = 8192
QTOT = 1536


def draw_queries(key, part):
    key = jax.random.fold_in(key, 11)
    normal_draw = jax.random.normal(key, (QTOT, HEADS * DL), jnp.float32)
    values = jnp.clip(normal_draw, -6.0, 6.0)
    return values.astype(jnp.bfloat16)


def draw_head_weights(key, part):
    key = jax.random.fold_in(key, 37)
    normal_draw = jax.random.normal(key, (QTOT, IHEADS), jnp.float32)
    values = jnp.clip(4.0 * normal_draw, -16.0, 16.0)
    return values


def draw_positions(key, part):
    key = jax.random.fold_in(key, 23)
    slot_index = jnp.arange(QTOT, dtype=jnp.int32)
    shard_index = slot_index // Q_DEV
    inner_index = slot_index % Q_DEV
    offset = jax.random.randint(key, (QTOT,), 0, TOK_DEV, dtype=jnp.int32)
    offset = jnp.where(inner_index == 0, 0, jnp.where(inner_index == 1, TOK_DEV - 1, offset))
    return (shard_index * TOK_DEV + offset).astype(jnp.int32)


def steps_of(rng, extent, shards, low, largest):
    loudness = 1.0
    for position, shards_of in shards:
        heights = jax.random.uniform(jax.random.fold_in(jax.random.fold_in(rng, 6), position), (shards_of,), jnp.float32, low / len(shards), largest / len(shards))
        loudness = loudness * jnp.repeat(jnp.exp(heights), extent[position] // shards_of).reshape((-1,) + (1,) * (len(extent) - 1 - position))
    return loudness


def noise(own_key, shape, scale, most, shards=(), kind=jnp.bfloat16):
    drawn = jax.random.normal(own_key, shape, jnp.float32) * scale
    if len(shards) > 0:
        drawn = steps_of(own_key, shape, shards, -0.22, 0.18) * drawn
    return jnp.clip(drawn, min=-most, max=most).astype(kind)


def setup_inputs(seed: int = 0) -> dict:
    key_of = jax.random.split(jax.random.key(seed), 7)
    return {
        "queries": draw_queries(jax.random.fold_in(key_of[6], 71), 0),
        "kv_latent": noise(key_of[1], (DL, TOKENS), 1.0, 6.0, ((1, 64),)),
        "index_queries": noise(key_of[2], (QTOT, IHEADS * DI), 1.0, 6.0, ((0, 64), (1, 4))),
        "index_keys": noise(key_of[3], (TOKENS, DI), 1.0, 6.0, ((0, 64),)),
        "head_weights": draw_head_weights(jax.random.fold_in(key_of[6], 71), 0),
        "positions": draw_positions(jax.random.fold_in(key_of[6], 71), 0),
    }


negative = -1e+30
loss_scale = 64.0
score_scale = 1.0 / math.sqrt(192.0)
highest = lax.Precision.HIGHEST

def reference(queries, kv_latent, index_queries, index_keys, head_weights, positions):
    key_positions = jnp.arange(TOKENS, dtype=jnp.int32)
    visible = key_positions[None, :] <= positions[:, None]
    latent_keys = kv_latent.astype(jnp.float32)
    query_heads = jnp.swapaxes(queries.astype(jnp.float32).reshape(QTOT, HEADS, DL), 0, 1)

    def head_probs(running, q_head):
        scores = jnp.dot(q_head, latent_keys, precision=highest) * score_scale
        scores = jnp.where(visible, scores, negative)
        row_max = lax.optimization_barrier(jnp.max(scores, axis=1, keepdims=True))
        expo_terms = jnp.where(visible, jnp.exp(scores - row_max), 0.0)
        return (running + expo_terms / lax.optimization_barrier(jnp.sum(expo_terms, axis=1, keepdims=True)), None)
    summed, _ = lax.scan(head_probs, jnp.zeros((QTOT, TOKENS), jnp.float32), query_heads)
    target = summed / HEADS
    coeff = 1.0 / math.sqrt(IHEADS * DI)
    keys_float = index_keys.astype(jnp.float32)
    index_heads = jnp.swapaxes(index_queries.astype(jnp.float32).reshape(QTOT, IHEADS, DI), 0, 1)
    weight_cols = jnp.transpose(head_weights)

    def logit_step(running, inputs):
        q_head, w_col = inputs
        inner = jnp.dot(q_head, keys_float.T, precision=highest)
        return (running + w_col[:, None] * jnp.maximum(inner, 0.0), None)
    weighted, _ = lax.scan(logit_step, jnp.zeros((QTOT, TOKENS), jnp.float32), (index_heads, weight_cols))
    logits = jnp.where(visible, coeff * weighted, negative)
    row_top = lax.optimization_barrier(jnp.max(logits, axis=1, keepdims=True))
    expo_logits = jnp.where(visible, jnp.exp(logits - row_top), 0.0)
    predicted = expo_logits / lax.optimization_barrier(jnp.sum(expo_logits, axis=1, keepdims=True))
    grad_logits = jnp.where(visible, loss_scale * (predicted - target), 0.0).astype(jnp.bfloat16)
    grad_values = lax.optimization_barrier(grad_logits).astype(jnp.float32)

    def back_step(running, inputs):
        q_head, w_col = inputs
        inner = jnp.dot(q_head, keys_float.T, precision=highest)
        head_grads = jnp.where(inner > 0.0, (coeff * w_col)[:, None] * grad_values, 0.0).astype(jnp.bfloat16)
        head_grads = lax.optimization_barrier(head_grads).astype(jnp.float32)
        query_grad = jnp.dot(head_grads, keys_float, precision=highest)
        return (running + jnp.dot(head_grads.T, q_head, precision=highest), query_grad)
    grad_keys, query_grads = lax.scan(back_step, jnp.zeros((TOKENS, DI), jnp.float32), (index_heads, weight_cols))
    grad_queries = jnp.swapaxes(query_grads, 0, 1).reshape(QTOT, IHEADS * DI)
    return (grad_queries, grad_keys)
```

```python
import math

import jax
import jax.numpy as jnp
from jax import lax
from jax.experimental import pallas as pl
from jax.experimental.pallas import tpu as pltpu
from jax.sharding import Mesh, PartitionSpec as P

DL = 576
HEADS = 64
IHEADS = 64
DI = 128
ROWS = 24
KPAD = 640
LOCAL = 16
RH = ROWS * HEADS
BLOCK = 384
KEYS = 2048

negative = -1e30
loss_scale = 64.0
score_scale = 1.0 / math.sqrt(192.0)
expo_scale = score_scale / math.log(2.0)
log2e = 1.0 / math.log(2.0)
coeff = 1.0 / math.sqrt(IHEADS * DI)

CTX = ("z", "yl", "x")
HEAD = ("yh", "core")
f32 = jnp.float32
bf16 = jnp.bfloat16


def nt(left, right):
    return lax.dot_general(left, right, (((1,), (1,)), ((), ())), preferred_element_type=f32)


def nn(left, right):
    return lax.dot_general(left, right, (((1,), (0,)), ((), ())), preferred_element_type=f32)


def weight_of(q_block):
    parts = q_block[:, DL : DL + 3].astype(f32)
    return parts[:, 0:1] + parts[:, 1:2] + parts[:, 2:3]


def forward_kernel(pos_ref, kpos_ref, q_ref, kk_ref, e_ref, logit_ref, stat_ref, bias, stat, acc):
    step = pl.program_id(0)
    keys = kk_ref.shape[0]

    @pl.when(step == 0)
    def _():
        bias[...] = jnp.where(kpos_ref[...] <= pos_ref[...], 0.0, negative)
        acc[...] = jnp.zeros_like(acc)

    heads = BLOCK // ROWS
    scores = nt(q_ref[:, :KPAD], kk_ref[:, :KPAD])
    scores = (scores.reshape(heads, ROWS, keys) + bias[...][None]).reshape(BLOCK, keys)
    best = jnp.max(scores, axis=1, keepdims=True)
    expo = jnp.exp2((scores - best) * expo_scale)
    total = jnp.sum(expo, axis=1, keepdims=True)
    e_ref[...] = expo.astype(bf16)
    lane = lax.broadcasted_iota(jnp.int32, (BLOCK, 128), 1)
    stat[pl.ds(step * BLOCK, BLOCK), :] = jnp.where(lane == 0, best, jnp.where(lane == 1, total, 0.0))
    inner = nt(q_ref[:, KPAD:], kk_ref[:, KPAD:])
    weighted = jnp.maximum(inner, 0.0) * weight_of(q_ref[:, :KPAD])
    acc[...] += jnp.sum(weighted.reshape(heads, ROWS, keys), axis=0)

    @pl.when(step == pl.num_programs(0) - 1)
    def _():
        logits = coeff * acc[...]
        logit_ref[...] = logits
        masked = logits + bias[...]
        top = jnp.max(masked, axis=1, keepdims=True)
        expo_sum = jnp.sum(jnp.exp2((masked - top) * log2e), axis=1, keepdims=True)
        small_lane = lax.broadcasted_iota(jnp.int32, (ROWS, 128), 1)
        stat[RH : RH + ROWS, :] = jnp.where(
            small_lane == 0, top, jnp.where(small_lane == 1, expo_sum, 0.0)
        )
        stat[RH + ROWS :, :] = jnp.zeros((128 - ROWS, 128), f32)
        stat_ref[...] = jnp.transpose(stat[...])[0:8, :]


def forward(positions, kpos, q_all, kk):
    keys = kk.shape[0]
    return pl.pallas_call(
        forward_kernel,
        grid=(RH // BLOCK,),
        in_specs=[
            pl.BlockSpec((ROWS, 1), lambda i: (0, 0)),
            pl.BlockSpec((1, keys), lambda i: (0, 0)),
            pl.BlockSpec((BLOCK, KPAD + DI), lambda i: (i, 0)),
            pl.BlockSpec((keys, KPAD + DI), lambda i: (0, 0)),
        ],
        out_specs=[
            pl.BlockSpec((BLOCK, keys), lambda i: (i, 0)),
            pl.BlockSpec((ROWS, keys), lambda i: (0, 0)),
            pl.BlockSpec((8, RH + 128), lambda i: (0, 0)),
        ],
        out_shape=[
            jax.ShapeDtypeStruct((RH, keys), bf16),
            jax.ShapeDtypeStruct((ROWS, keys), f32),
            jax.ShapeDtypeStruct((8, RH + 128), f32),
        ],
        scratch_shapes=[
            pltpu.VMEM((ROWS, keys), f32),
            pltpu.VMEM((RH + 128, 128), f32),
            pltpu.VMEM((ROWS, keys), f32),
        ],
        compiler_params=pltpu.CompilerParams(vmem_limit_bytes=56 * 1024 * 1024),
        cost_estimate=pl.CostEstimate(
            flops=2 * RH * keys * 768, bytes_accessed=2 * RH * keys, transcendentals=RH * keys
        ),
        name="forward",
    )(positions, kpos, q_all, kk)


def backward_kernel(
    pos_ref, kpos_ref, own_ref, others_ref, e_ref, logit_ref, q_ref, kk_ref, dq_ref, dk_ref, factor, target, grad, dkt
):
    step = pl.program_id(0)
    half = pl.num_programs(0) // 2
    keys = kk_ref.shape[0]
    heads = BLOCK // ROWS

    @pl.when(step == 0)
    def _():
        best = own_ref[0:1, :]
        gbest = best
        for j in range(3):
            gbest = jnp.maximum(gbest, others_ref[j, 0:1, :])
        is_logit = lax.broadcasted_iota(jnp.int32, (1, RH + 128), 1) >= RH
        scale = jnp.where(is_logit, log2e, expo_scale)
        total = own_ref[1:2, :] * jnp.exp2((best - gbest) * scale)
        for j in range(3):
            total += others_ref[j, 1:2, :] * jnp.exp2((others_ref[j, 0:1, :] - gbest) * scale)
        own_factor = jnp.where(is_logit, 1.0, jnp.exp2((best - gbest) * scale) / HEADS) / total
        rows = lax.broadcasted_iota(jnp.int32, (8, RH + 128), 0)
        packed = jnp.where(rows == 0, own_factor, jnp.where(rows == 1, gbest, 0.0))
        packed = jnp.concatenate([packed, jnp.zeros((120, RH + 128), f32)], axis=0)
        factor[...] = jnp.transpose(packed)
        target[...] = jnp.zeros_like(target)

    @pl.when(step < half)
    def _():
        start = pl.multiple_of(step * BLOCK, BLOCK)
        scaled = e_ref[...].astype(f32) * factor[pl.ds(start, BLOCK), 0:1]
        target[...] += jnp.sum(scaled.reshape(heads, ROWS, keys), axis=0)

    @pl.when(step == half - 1)
    def _():
        top = factor[RH : RH + ROWS, 1:2]
        inverse = factor[RH : RH + ROWS, 0:1]
        visible = kpos_ref[...] <= pos_ref[...]
        masked = jnp.where(visible, logit_ref[...], negative)
        predicted = jnp.exp2((masked - top) * log2e) * inverse
        value = jnp.where(visible, loss_scale * (predicted - target[...]), 0.0)
        grad[...] = value.astype(bf16).astype(f32)
        dkt[...] = jnp.zeros_like(dkt)

    @pl.when(step >= half)
    def _():
        keys_mat = kk_ref[:, KPAD:]
        iq = q_ref[:, KPAD:]
        inner = nt(iq, keys_mat)
        weight = coeff * weight_of(q_ref[:, :KPAD])
        spread = jnp.broadcast_to(grad[...][None], (heads, ROWS, keys)).reshape(BLOCK, keys)
        head_grads = jnp.where(inner > 0.0, weight * spread, 0.0).astype(bf16)
        dq = nn(head_grads, keys_mat)
        for j in range(heads):
            dq_ref[0, :, j * DI : (j + 1) * DI] = dq[j * ROWS : (j + 1) * ROWS].astype(bf16)
        dkt[...] += nn(jnp.transpose(iq), head_grads)

    @pl.when(step == 2 * half - 1)
    def _():
        dk_ref[...] = jnp.transpose(dkt[...]).astype(bf16)


def backward(positions, kpos, own, others, expo, logits, q_all, kk):
    keys = kk.shape[0]
    half = RH // BLOCK
    first = lambda i: jnp.minimum(i, half - 1)
    second = lambda i: jnp.maximum(i - half, 0)
    return pl.pallas_call(
        backward_kernel,
        grid=(2 * half,),
        in_specs=[
            pl.BlockSpec((ROWS, 1), lambda i: (0, 0)),
            pl.BlockSpec((1, keys), lambda i: (0, 0)),
            pl.BlockSpec((8, RH + 128), lambda i: (0, 0)),
            pl.BlockSpec((3, 8, RH + 128), lambda i: (0, 0, 0)),
            pl.BlockSpec((BLOCK, keys), lambda i: (first(i), 0)),
            pl.BlockSpec((ROWS, keys), lambda i: (0, 0)),
            pl.BlockSpec((BLOCK, KPAD + DI), lambda i: (second(i), 0)),
            pl.BlockSpec((keys, KPAD + DI), lambda i: (0, 0)),
        ],
        out_specs=[
            pl.BlockSpec((1, ROWS, LOCAL * DI), lambda i: (second(i), 0, 0)),
            pl.BlockSpec((keys, DI), lambda i: (0, 0)),
        ],
        out_shape=[
            jax.ShapeDtypeStruct((4, ROWS, LOCAL * DI), bf16),
            jax.ShapeDtypeStruct((keys, DI), bf16),
        ],
        scratch_shapes=[
            pltpu.VMEM((RH + 128, 128), f32),
            pltpu.VMEM((ROWS, keys), f32),
            pltpu.VMEM((ROWS, keys), f32),
            pltpu.VMEM((DI, keys), f32),
        ],
        compiler_params=pltpu.CompilerParams(vmem_limit_bytes=56 * 1024 * 1024),
        cost_estimate=pl.CostEstimate(
            flops=6 * RH * keys * 128, bytes_accessed=2 * RH * keys, transcendentals=0
        ),
        name="backward",
    )(positions, kpos, own, others, expo, logits, q_all, kk)


def flip(value, axis):
    return lax.ppermute(value, axis, [(0, 1), (1, 0)])


def head_xor(value, bits):
    return lax.ppermute(value, HEAD, [(i, i ^ bits) for i in range(4)])


def body(queries, kv_latent, index_queries, index_keys, head_weights, positions):
    z, yl, x = (lax.axis_index(a) for a in CTX)
    head = lax.axis_index(HEAD)
    with jax.named_scope("local_prep"):
        own_keys = jnp.concatenate(
            [
                jnp.transpose(lax.dynamic_slice_in_dim(kv_latent, head * 32, 32, 1)),
                jnp.zeros((32, KPAD - DL), bf16),
                lax.dynamic_slice_in_dim(index_keys, head * 32, 32, 0),
            ],
            axis=1,
        )
        w = jnp.transpose(head_weights).reshape(LOCAL * ROWS, 1)
        hi = lax.reduce_precision(w, 8, 7)
        mid = lax.reduce_precision(w - hi, 8, 7)
        low = w - hi - mid
        q_own = jnp.concatenate(
            [
                jnp.transpose(queries.reshape(ROWS, LOCAL, DL), (1, 0, 2)).reshape(LOCAL * ROWS, DL),
                hi.astype(bf16),
                mid.astype(bf16),
                low.astype(bf16),
                jnp.zeros((LOCAL * ROWS, KPAD - DL - 3), bf16),
                jnp.transpose(index_queries.reshape(ROWS, LOCAL, DI), (1, 0, 2)).reshape(
                    LOCAL * ROWS, DI
                ),
            ],
            axis=1,
        )
    with jax.named_scope("gather_queries"):
        q_yh = flip(q_own, "yh")
        q_core = flip(q_own, "core")
        q_both = flip(q_yh, "core")
        q_all = jnp.concatenate([q_own, q_core, q_yh, q_both], axis=0)
    with jax.named_scope("gather_keys"):
        over_z = lax.all_to_all(
            jnp.broadcast_to(own_keys[None], (8, 32, KPAD + DI)), "z", 0, 0, tiled=True
        ).reshape(256, KPAD + DI)
        over_y = jnp.concatenate([over_z, flip(over_z, "yl")], axis=0)
        pieces = [over_y] + [
            lax.ppermute(over_y, "x", [((i + s) % 4, i) for i in range(4)]) for s in (1, 2, 3)
        ]
        kk = jnp.concatenate(pieces, axis=0)
    index = jnp.arange(KEYS, dtype=jnp.int32)
    slot_x = (x + index // 512) % 4
    slot_y = (yl + (index // 256) % 2) % 2
    slot_z = (index // 32) % 8
    kpos = ((slot_z * 8 + slot_y * 4 + slot_x) * 128 + head * 32 + index % 32)[None, :]
    pos = positions[:, None]
    expo, logits, stats = forward(pos, kpos, q_all, kk)
    with jax.named_scope("exchange_stats"):
        others = []
        for bits in (1, 2, 3):
            got = head_xor(stats, bits)
            groups = [got[:, (s ^ bits) * 384 : (s ^ bits) * 384 + 384] for s in range(4)]
            others.append(jnp.concatenate(groups + [got[:, RH:]], axis=1))
        others = jnp.stack(others)
    dq, dk = backward(pos, kpos, stats, others, expo, logits, q_all, kk)
    with jax.named_scope("reduce_keys"):
        got = [
            lax.ppermute(dk[512 * s : 512 * s + 512], "x", [(i, (i + s) % 4) for i in range(4)])
            for s in (1, 2, 3)
        ]
        dk_x = dk[:512].astype(f32)
        for part in got:
            dk_x = dk_x + part.astype(f32)
        away = flip(dk_x[256:].astype(bf16), "yl")
        dk_y = dk_x[:256] + away.astype(f32)
        dk_z = lax.all_to_all(dk_y.astype(bf16).reshape(8, 32, DI), "z", 0, 0, tiled=True)
        grad_keys = jnp.sum(dk_z.astype(f32), axis=0)
    with jax.named_scope("reduce_queries"):
        grad_queries = dq[0].astype(f32)
        for bits in (1, 2, 3):
            grad_queries = grad_queries + head_xor(dq[bits], bits).astype(f32)
    return (grad_queries, grad_keys)


def solution(mesh):
    fine = Mesh(mesh.devices.reshape(8, 2, 4, 2, 2), CTX + HEAD)
    in_specs = (
        P(CTX, HEAD),
        P(None, CTX),
        P(CTX, HEAD),
        P(CTX, None),
        P(CTX, HEAD),
        P(CTX),
    )
    out_specs = (P(CTX, HEAD), P(CTX + HEAD, None))
    return jax.shard_map(body, mesh=fine, in_specs=in_specs, out_specs=out_specs, check_vma=False)
```

```python
import functools
import math

import jax
import jax.numpy as jnp
from jax import lax
from jax.experimental import pallas as pl
from jax.experimental.pallas import tpu as pltpu
from jax.sharding import Mesh, PartitionSpec as P

DL = 576
HEADS = 64
IHEADS = 64
DI = 128
ROWS = 24
KPAD = 640
LOCAL = 16
RH = ROWS * HEADS
BLOCK = 384
KEYS = 2048
PIECE = 256
STATS = RH + 128
IQ_AT = LOCAL * DL
W_AT = IQ_AT + LOCAL * DI
RAW = W_AT + 128
FORWARD_SPLIT = True
BACKWARD_STARTS = (0, 2, 5)
VMEM_LIMIT = 28 * 1024 * 1024

negative = -1e30
loss_scale = 64.0
score_scale = 1.0 / math.sqrt(192.0)
expo_scale = score_scale / math.log(2.0)
log2e = 1.0 / math.log(2.0)
coeff = 1.0 / math.sqrt(IHEADS * DI)

CTX = ("z", "yl", "x")
HEAD = ("yh", "core")
f32 = jnp.float32
bf16 = jnp.bfloat16


def nt(left, right):
    return lax.dot_general(left, right, (((1,), (1,)), ((), ())), preferred_element_type=f32)


def nn(left, right):
    return lax.dot_general(left, right, (((1,), (0,)), ((), ())), preferred_element_type=f32)


def weight_of(q_block, at=DL):
    parts = q_block[:, at : at + 3].astype(f32)
    return parts[:, 0:1] + parts[:, 1:2] + parts[:, 2:3]


def is_logit_row():
    return lax.broadcasted_iota(jnp.int32, (1, STATS), 1) >= RH


def scale_row():
    return jnp.where(is_logit_row(), log2e, expo_scale)


def merge(pairs):
    best = pairs[0][0]
    for other, _ in pairs[1:]:
        best = jnp.maximum(best, other)
    total = None
    for other, part in pairs:
        term = part * jnp.exp2((other - best) * scale_row())
        total = term if total is None else total + term
    return best, total


def assemble_kernel(*refs):
    raws, q_ref = refs[:4], refs[4]
    lane = lax.broadcasted_iota(jnp.int32, (ROWS, 128), 1)
    for b in range(4):
        weights = raws[b][:, W_AT : W_AT + 128].astype(f32)
        for pair in range(LOCAL // 2):
            rows = []
            for j in (2 * pair, 2 * pair + 1):
                start = j * DL - (j % 2) * 64
                wide = raws[b][:, start : start + KPAD].astype(f32)
                if j % 2:
                    wide = pltpu.roll(wide, KPAD - 64, 1)
                held = pltpu.roll(weights, (64 - 8 * j) % 128, 1)
                last = jnp.where(lane < 64, wide[:, 512:], jnp.where(lane < 67, held, 0.0))
                iq = raws[b][:, IQ_AT + j * DI : IQ_AT + (j + 1) * DI].astype(f32)
                rows.append(jnp.concatenate([wide[:, :512], last, iq], axis=1))
            at = (b * LOCAL + 2 * pair) * ROWS
            q_ref[at : at + 2 * ROWS, :] = jnp.concatenate(rows, axis=0).astype(bf16)


def assemble(raws):
    return pl.pallas_call(
        assemble_kernel,
        grid=(1,),
        in_specs=[pl.BlockSpec((ROWS, RAW), lambda i: (0, 0))] * 4,
        out_specs=pl.BlockSpec((RH, KPAD + DI), lambda i: (0, 0)),
        out_shape=jax.ShapeDtypeStruct((RH, KPAD + DI), bf16),
        compiler_params=pltpu.CompilerParams(vmem_limit_bytes=VMEM_LIMIT),
        cost_estimate=pl.CostEstimate(flops=0, bytes_accessed=5000000, transcendentals=0),
        name="assemble",
    )(*raws)


def key_positions(base):
    lane = lax.broadcasted_iota(jnp.int32, (1, PIECE), 1)
    return base + (lane // 32) * 1024 + lane % 32


class Copies:
    def __init__(self, sems):
        self.sems, self.used = sems, 0

    def make(self, source, target):
        copy = pltpu.make_async_copy(source, target, self.sems.at[self.used])
        self.used += 1
        return copy


def forward_kernel(count, first, *refs):
    base_ref, pos_ref, prev_ref, q_ref = refs[:4]
    pieces = refs[4 : 4 + count]
    e_hbm, logit_hbm, stat_ref, keys_hbm = refs[4 + count : 8 + count]
    expos, logits, stat, sems = refs[8 + count :]
    copies = Copies(sems)
    weight = weight_of(q_ref[:, :KPAD])
    stores = []

    def store(source, target):
        copy = copies.make(source, target)
        copy.start()
        stores.append(copy)

    done = 0
    for j in range(count):
        kpos = key_positions(base_ref[first + j])
        bias = jnp.where(kpos <= pos_ref[:, 0:1], 0.0, negative)
        part = nt(q_ref[:, :KPAD], pieces[j][:, :KPAD])
        inner = nt(q_ref[:, KPAD:], pieces[j][:, KPAD:])
        part = (part.reshape(HEADS, ROWS, PIECE) + bias[None]).reshape(RH, PIECE)
        best = jnp.max(part, axis=1, keepdims=True)
        weighted = jnp.maximum(inner, 0.0) * weight
        logit = coeff * jnp.sum(weighted.reshape(HEADS, ROWS, PIECE), axis=0)
        logits[j] = logit
        expo = jnp.exp2((part - best) * expo_scale)
        expos[j] = expo.astype(bf16)
        stat[:RH, 2 * j : 2 * j + 1] = best
        stat[:RH, 2 * j + 1 : 2 * j + 2] = jnp.sum(expo, axis=1, keepdims=True)
        masked = logit + bias
        top = jnp.max(masked, axis=1, keepdims=True)
        stat[RH : RH + ROWS, 2 * j : 2 * j + 1] = top
        stat[RH : RH + ROWS, 2 * j + 1 : 2 * j + 2] = jnp.sum(
            jnp.exp2((masked - top) * log2e), axis=1, keepdims=True
        )
        if j + 1 == count or (count - j - 1) % 2 == 0 and FORWARD_SPLIT:
            for i in range(done, j + 1):
                store(expos.at[i], e_hbm.at[i])
                store(logits.at[i], logit_hbm.at[i])
                store(pieces[i].at[:, pl.ds(KPAD, DI)], keys_hbm.at[i])
            done = j + 1
    stat[RH + ROWS :, :] = jnp.zeros((128 - ROWS, 128), f32)
    turned = jnp.transpose(stat[...])
    pairs = [(turned[2 * j : 2 * j + 1], turned[2 * j + 1 : 2 * j + 2]) for j in range(count)]
    best, total = merge([(prev_ref[0:1, :], prev_ref[1:2, :])] + pairs)
    rows = [best, total] + [p[0] for p in pairs]
    if len(rows) < 8:
        rows.append(jnp.zeros((8 - len(rows), STATS), f32))
    stat_ref[...] = jnp.concatenate(rows, axis=0)
    for copy in stores:
        copy.wait()


def forward(bases, first, positions, prev, q_all, pieces):
    count = len(pieces)
    keys = PIECE * count
    hbm = pl.BlockSpec(memory_space=pl.ANY)
    vmem = pl.BlockSpec(memory_space=pltpu.VMEM)
    return pl.pallas_call(
        functools.partial(forward_kernel, count, first),
        in_specs=[pl.BlockSpec(memory_space=pltpu.SMEM)] + [vmem] * (3 + count),
        out_specs=[hbm, hbm, vmem, hbm],
        out_shape=[
            jax.ShapeDtypeStruct((count, RH, PIECE), bf16),
            jax.ShapeDtypeStruct((count, ROWS, PIECE), f32),
            jax.ShapeDtypeStruct((8, STATS), f32),
            jax.ShapeDtypeStruct((count, PIECE, DI), bf16),
        ],
        scratch_shapes=[
            pltpu.VMEM((count, RH, PIECE), bf16),
            pltpu.VMEM((count, ROWS, PIECE), f32),
            pltpu.VMEM((STATS, 128), f32),
            pltpu.SemaphoreType.DMA((3 * count,)),
        ],
        compiler_params=pltpu.CompilerParams(vmem_limit_bytes=VMEM_LIMIT),
        cost_estimate=pl.CostEstimate(
            flops=2 * RH * keys * 1536, bytes_accessed=2 * RH * keys, transcendentals=RH * keys
        ),
        name="forward",
    )(bases, positions, prev, q_all, *pieces)


def backward_keys_kernel(sizes, *refs):
    n = len(sizes)
    place_ref, base_ref, pos_ref = refs[:3]
    stats = refs[3 : 6 + n]
    e_hbm = refs[6 + n : 6 + 2 * n]
    logit_hbm = refs[6 + 2 * n : 6 + 3 * n]
    key_hbm = refs[6 + 3 * n : 6 + 4 * n]
    q_ref = refs[6 + 4 * n]
    dk_hbm, grad_hbm, keys_hbm = refs[7 + 4 * n : 10 + 4 * n]
    rest = refs[10 + 4 * n :]
    factor, expos, logits, keys_ref, dk_ref, grad_ref, sems = rest
    count = sum(sizes)
    flat = [(j, i) for j in range(n) for i in range(sizes[j])]
    copies = Copies(sems)
    load_e = [copies.make(e_hbm[j].at[i], expos.at[k]) for k, (j, i) in enumerate(flat)]
    load_logits = [copies.make(logit_hbm[j].at[i], logits.at[k]) for k, (j, i) in enumerate(flat)]
    load_keys = [copies.make(key_hbm[j].at[i], keys_ref.at[k]) for k, (j, i) in enumerate(flat)]

    def fetch(k):
        for load in (load_e[k], load_logits[k], load_keys[k]):
            load.start()

    for k in range(count):
        fetch(k)
    stores = []

    def store(source, target):
        copy = copies.make(source, target)
        copy.start()
        stores.append(copy)

    other_refs = stats[:3]
    stat_refs = stats[3:]
    pairs = [(stat_refs[n - 1][0:1, :], stat_refs[n - 1][1:2, :])]
    for bits in (1, 2, 3):
        got = other_refs[bits - 1]
        pair = []
        for r in range(2):
            parts = [got[r : r + 1, (s ^ bits) * 384 : (s ^ bits) * 384 + 384] for s in range(4)]
            pair.append(jnp.concatenate(parts + [got[r : r + 1, RH:]], axis=1))
        pairs.append(tuple(pair))
    gbest, total = merge(pairs)
    inverse = 1.0 / total
    rows = [inverse, gbest]
    for j, i in flat:
        rows.append(
            jnp.exp2((stat_refs[j][2 + i : 3 + i, :] - gbest) * expo_scale)
            * (inverse * (1.0 / HEADS))
        )
    rows.append(jnp.zeros((128 - len(rows), STATS), f32))
    factor[...] = jnp.transpose(jnp.concatenate(rows, axis=0))
    top = factor[RH : RH + ROWS, 1:2]
    inverse = factor[RH : RH + ROWS, 0:1]
    repeat = (
        lax.broadcasted_iota(jnp.int32, (ROWS, BLOCK), 1) % ROWS
        == lax.broadcasted_iota(jnp.int32, (ROWS, BLOCK), 0)
    ).astype(bf16)
    weight_rows = jnp.transpose(jnp.broadcast_to(coeff * weight_of(q_ref[:, :KPAD]), (RH, 128)))[0:1, :]
    done = 0
    for k in range(count):
        if k in BACKWARD_STARTS:
            upto = min([i for i in BACKWARD_STARTS if i > k] + [count])
            for i in range(k, upto):
                for load in (load_e[i], load_logits[i], load_keys[i]):
                    load.wait()
        scaled = expos[k].astype(f32) * factor[:RH, 2 + k : 3 + k]
        target = jnp.sum(scaled.reshape(HEADS, ROWS, PIECE), axis=0)
        visible = key_positions(base_ref[k]) <= pos_ref[:, 0:1]
        masked = jnp.where(visible, logits[k], negative)
        predicted = jnp.exp2((masked - top) * log2e) * inverse
        value = jnp.where(visible, loss_scale * (predicted - target), 0.0)
        rounded = value.astype(bf16)
        grad_ref[k] = rounded.astype(f32)
        spread = tn(rounded, repeat)
        dk = None
        for r in range(RH // BLOCK):
            iq = q_ref[r * BLOCK : (r + 1) * BLOCK, KPAD:]
            inner = nt(keys_ref[k], iq)
            weight = weight_rows[:, r * BLOCK : (r + 1) * BLOCK]
            head_grads = jnp.where(inner > 0.0, spread * weight, 0.0).astype(bf16)
            term = nn(head_grads, iq)
            dk = term if dk is None else dk + term
        dk_ref[k] = dk.astype(bf16)
        if k + 1 in BACKWARD_STARTS or k + 1 == count:
            for i in range(done, k + 1):
                store(dk_ref.at[i], dk_hbm.at[place_ref[i]])
                store(grad_ref.at[i], grad_hbm.at[:, pl.ds(i * PIECE, PIECE)])
                store(keys_ref.at[i], keys_hbm.at[pl.ds(i * PIECE, PIECE)])
            done = k + 1
    for copy in stores:
        copy.wait()


def tn(left, right):
    return lax.dot_general(left, right, (((0,), (0,)), ((), ())), preferred_element_type=f32)


def head_grads_of(q_ref, keys_mat, grad):
    heads = BLOCK // ROWS
    keys = keys_mat.shape[0]
    inner = nt(q_ref[:, KPAD:], keys_mat)
    weight = coeff * weight_of(q_ref[:, :KPAD])
    spread = jnp.broadcast_to(grad[None], (heads, ROWS, keys)).reshape(BLOCK, keys)
    return jnp.where(inner > 0.0, weight * spread, 0.0).astype(bf16)


def backward_keys(place, bases, positions, others, stats, expos, logits, keys_list, q_all):
    sizes = tuple(e.shape[0] for e in expos)
    count = sum(sizes)
    keys = PIECE * count
    hbm = pl.BlockSpec(memory_space=pl.ANY)
    vmem = pl.BlockSpec(memory_space=pltpu.VMEM)
    smem = pl.BlockSpec(memory_space=pltpu.SMEM)
    return pl.pallas_call(
        functools.partial(backward_keys_kernel, sizes),
        in_specs=[smem, smem] + [vmem] * (4 + len(sizes)) + [hbm] * (3 * len(sizes)) + [vmem],
        out_specs=[hbm] * 3,
        scratch_shapes=[
            pltpu.VMEM((STATS, 128), f32),
            pltpu.VMEM((count, RH, PIECE), bf16),
            pltpu.VMEM((count, ROWS, PIECE), f32),
            pltpu.VMEM((count, PIECE, DI), bf16),
            pltpu.VMEM((count, PIECE, DI), bf16),
            pltpu.VMEM((count, ROWS, PIECE), f32),
            pltpu.SemaphoreType.DMA((6 * count,)),
        ],
        out_shape=[
            jax.ShapeDtypeStruct((count, PIECE, DI), bf16),
            jax.ShapeDtypeStruct((ROWS, keys), f32),
            jax.ShapeDtypeStruct((keys, DI), bf16),
        ],
        compiler_params=pltpu.CompilerParams(vmem_limit_bytes=VMEM_LIMIT),
        cost_estimate=pl.CostEstimate(
            flops=8 * RH * keys * 128, bytes_accessed=2 * RH * keys, transcendentals=0
        ),
        name="backward_keys",
    )(place, bases, positions, *others, *stats, *expos, *logits, *keys_list, q_all)


def backward_queries_kernel(q_ref, keys_ref, grad_ref, dq_ref):
    dq = nn(head_grads_of(q_ref, keys_ref[...], grad_ref[...]), keys_ref[...])
    for j in range(BLOCK // ROWS):
        dq_ref[0, :, j * DI : (j + 1) * DI] = dq[j * ROWS : (j + 1) * ROWS].astype(bf16)


def backward_queries(q_all, iqkeys, grad):
    keys = iqkeys.shape[0]
    return pl.pallas_call(
        backward_queries_kernel,
        grid=(RH // BLOCK,),
        in_specs=[
            pl.BlockSpec((BLOCK, KPAD + DI), lambda i: (i, 0)),
            pl.BlockSpec((keys, DI), lambda i: (0, 0)),
            pl.BlockSpec((ROWS, keys), lambda i: (0, 0)),
        ],
        out_specs=pl.BlockSpec((1, ROWS, LOCAL * DI), lambda i: (i, 0, 0)),
        out_shape=jax.ShapeDtypeStruct((4, ROWS, LOCAL * DI), bf16),
        compiler_params=pltpu.CompilerParams(vmem_limit_bytes=VMEM_LIMIT),
        cost_estimate=pl.CostEstimate(
            flops=8 * RH * keys * 128, bytes_accessed=2 * RH * keys, transcendentals=0
        ),
        name="backward_queries",
    )(q_all, iqkeys, grad)


def flip(value, axis):
    return lax.ppermute(value, axis, [(0, 1), (1, 0)])


def head_xor(value, bits):
    return lax.ppermute(value, HEAD, [(i, i ^ bits) for i in range(4)])


def body(queries, kv_latent, index_queries, index_keys, head_weights, positions):
    z, yl, x = (lax.axis_index(a) for a in CTX)
    head = lax.axis_index(HEAD)
    with jax.named_scope("own_keys"):
        own_keys = jnp.concatenate(
            [
                jnp.transpose(lax.dynamic_slice_in_dim(kv_latent, head * 32, 32, 1)),
                jnp.zeros((32, KPAD - DL), bf16),
                lax.dynamic_slice_in_dim(index_keys, head * 32, 32, 0),
            ],
            axis=1,
        )
        own_keys = jnp.broadcast_to(own_keys[None], (8, 32, KPAD + DI))
        own_keys, queries, index_queries, head_weights = lax.optimization_barrier(
            (own_keys, queries, index_queries, head_weights)
        )
    with jax.named_scope("own_queries"):
        w = head_weights
        hi = lax.reduce_precision(w, 8, 7)
        mid = lax.reduce_precision(w - hi, 8, 7)
        low = w - hi - mid
        w_parts = jnp.stack([hi, mid, low] + [jnp.zeros_like(w)] * 5, axis=2).astype(bf16)
        q_own = jnp.concatenate([queries, index_queries, w_parts.reshape(ROWS, 128)], axis=1)
    with jax.named_scope("gather_queries"):
        q_yh = flip(q_own, "yh")
        q_core = flip(q_own, "core")
        q_both = flip(q_yh, "core")
        q_all = assemble([q_own, q_core, q_yh, q_both])

    def shift(value, s):
        return lax.ppermute(value, "x", [((i + s) % 4, i) for i in range(4)])

    with jax.named_scope("gather_keys"):
        p00 = lax.all_to_all(own_keys, "z", 0, 0, tiled=True).reshape(PIECE, KPAD + DI)
        p00, q_all = lax.optimization_barrier((p00, q_all))
        p01 = flip(p00, "yl")
        p10, p30 = shift(p00, 1), shift(p00, 3)
        p20 = shift(p00, 2)
        p11, p31 = shift(p01, 1), shift(p01, 3)
        p21 = flip(p20, "yl")
    groups = [
        [(0, 0, p00), (1, 0, p10), (3, 0, p30), (0, 1, p01), (2, 0, p20)],
        [(1, 1, p11), (3, 1, p31), (2, 1, p21)],
    ]
    flat = [entry for group in groups for entry in group]
    place = jnp.stack([((yl + b) % 2) * 4 + (x + s) % 4 for s, b, _ in flat])
    bases = place * 128 + head * 32
    pos = jnp.broadcast_to(positions[:, None], (ROWS, 128))
    stat = jnp.concatenate(
        [jnp.full((1, STATS), negative, f32), jnp.zeros((7, STATS), f32)], axis=0
    )
    expos, logits, stats, keys_list = [], [], [], []
    first = 0
    for group in groups:
        expo, logit, stat, keys = forward(
            bases, first, pos, stat, q_all, [p for _, _, p in group]
        )
        first += len(group)
        expos.append(expo)
        logits.append(logit)
        stats.append(stat)
        keys_list.append(keys)
    with jax.named_scope("exchange_stats"):
        others = [head_xor(stat, bits) for bits in (1, 2, 3)]
    dk, grad, iqkeys = backward_keys(
        place, bases, pos, others, stats, expos, logits, keys_list, q_all
    )
    dq = backward_queries(q_all, iqkeys, grad)
    with jax.named_scope("reduce_keys"):
        dk_xy = lax.all_to_all(dk, ("yl", "x"), 0, 0, tiled=True)
        dk_xy = jnp.sum(dk_xy.astype(f32), axis=0).astype(bf16)
        dk_z = lax.all_to_all(dk_xy.reshape(8, 32, DI), "z", 0, 0, tiled=True)
        grad_keys = jnp.sum(dk_z.astype(f32), axis=0)
    with jax.named_scope("reduce_queries"):
        grad_queries = dq[0].astype(f32)
        for bits in (1, 2, 3):
            grad_queries = grad_queries + head_xor(dq[bits], bits).astype(f32)
    return (grad_queries, grad_keys)


def solution(mesh):
    fine = Mesh(mesh.devices.reshape(8, 2, 4, 2, 2), CTX + HEAD)
    in_specs = (
        P(CTX, HEAD),
        P(None, CTX),
        P(CTX, HEAD),
        P(CTX, None),
        P(CTX, HEAD),
        P(CTX),
    )
    out_specs = (P(CTX, HEAD), P(CTX + HEAD, None))
    return jax.shard_map(body, mesh=fine, in_specs=in_specs, out_specs=out_specs, check_vma=False)
```

```python
import functools
import math

import jax
import jax.numpy as jnp
from jax import lax
from jax.experimental import pallas as pl
from jax.experimental.pallas import tpu as pltpu
from jax.sharding import Mesh, PartitionSpec as P

DL = 576
HEADS = 64
IHEADS = 64
DI = 128
ROWS = 24
KPAD = 640
LOCAL = 16
RH = ROWS * HEADS
BLOCK = 384
KEYS = 2048
PIECE = 256
STATS = RH + 128
IQ_AT = LOCAL * DL
W_AT = IQ_AT + LOCAL * DI
RAW = W_AT + 128
VMEM_LIMIT = 28 * 1024 * 1024

negative = -1e30
loss_scale = 64.0
score_scale = 1.0 / math.sqrt(192.0)
expo_scale = score_scale / math.log(2.0)
log2e = 1.0 / math.log(2.0)
coeff = 1.0 / math.sqrt(IHEADS * DI)

CTX = ("z", "yl", "x")
HEAD = ("yh", "core")
f32 = jnp.float32
bf16 = jnp.bfloat16


def nt(left, right):
    return lax.dot_general(left, right, (((1,), (1,)), ((), ())), preferred_element_type=f32)


def nn(left, right):
    return lax.dot_general(left, right, (((1,), (0,)), ((), ())), preferred_element_type=f32)


def weight_of(q_block, at=DL):
    parts = q_block[:, at : at + 3].astype(f32)
    return parts[:, 0:1] + parts[:, 1:2] + parts[:, 2:3]


def is_logit_row():
    return lax.broadcasted_iota(jnp.int32, (1, STATS), 1) >= RH


def scale_row():
    return jnp.where(is_logit_row(), log2e, expo_scale)


def merge(pairs):
    best = pairs[0][0]
    for other, _ in pairs[1:]:
        best = jnp.maximum(best, other)
    total = None
    for other, part in pairs:
        term = part * jnp.exp2((other - best) * scale_row())
        total = term if total is None else total + term
    return best, total


def assemble_kernel(*refs):
    raws, q_ref = refs[:4], refs[4]
    lane = lax.broadcasted_iota(jnp.int32, (ROWS, 128), 1)
    for b in range(4):
        weights = raws[b][:, W_AT : W_AT + 128].astype(f32)
        for pair in range(LOCAL // 2):
            rows = []
            for j in (2 * pair, 2 * pair + 1):
                start = j * DL - (j % 2) * 64
                wide = raws[b][:, start : start + KPAD].astype(f32)
                if j % 2:
                    wide = pltpu.roll(wide, KPAD - 64, 1)
                held = pltpu.roll(weights, (64 - 8 * j) % 128, 1)
                last = jnp.where(lane < 64, wide[:, 512:], jnp.where(lane < 67, held, 0.0))
                iq = raws[b][:, IQ_AT + j * DI : IQ_AT + (j + 1) * DI].astype(f32)
                rows.append(jnp.concatenate([wide[:, :512], last, iq], axis=1))
            at = (b * LOCAL + 2 * pair) * ROWS
            q_ref[at : at + 2 * ROWS, :] = jnp.concatenate(rows, axis=0).astype(bf16)


def assemble(raws):
    return pl.pallas_call(
        assemble_kernel,
        grid=(1,),
        in_specs=[pl.BlockSpec((ROWS, RAW), lambda i: (0, 0))] * 4,
        out_specs=pl.BlockSpec((RH, KPAD + DI), lambda i: (0, 0)),
        out_shape=jax.ShapeDtypeStruct((RH, KPAD + DI), bf16),
        compiler_params=pltpu.CompilerParams(vmem_limit_bytes=VMEM_LIMIT),
        cost_estimate=pl.CostEstimate(flops=0, bytes_accessed=5000000, transcendentals=0),
        name="assemble",
    )(*raws)


def key_positions(base):
    lane = lax.broadcasted_iota(jnp.int32, (1, PIECE), 1)
    return base + (lane // 32) * 1024 + lane % 32


def forward_kernel(count, first, *refs):
    base_ref, pos_ref, prev_ref, q_ref = refs[:4]
    pieces = refs[4 : 4 + count]
    e_ref, logit_ref, keys_ref, stat_ref, stat = refs[4 + count :]
    weight = weight_of(q_ref[:, :KPAD])

    def products(j):
        part = nt(q_ref[:, :KPAD], pieces[j][:, :KPAD])
        inner = nt(q_ref[:, KPAD:], pieces[j][:, KPAD:])
        weighted = jnp.maximum(inner, 0.0) * weight
        return part, coeff * jnp.sum(weighted.reshape(HEADS, ROWS, PIECE), axis=0)

    ready = products(0)
    for j in range(count):
        part, logit = ready
        if j + 1 < count:
            ready = products(j + 1)
        kpos = key_positions(base_ref[first + j])
        bias = jnp.where(kpos <= pos_ref[:, 0:1], 0.0, negative)
        part = (part.reshape(HEADS, ROWS, PIECE) + bias[None]).reshape(RH, PIECE)
        best = jnp.max(part, axis=1, keepdims=True)
        logit_ref[j] = logit
        expo = jnp.exp2((part - best) * expo_scale)
        e_ref[j] = expo.astype(bf16)
        stat[:RH, 2 * j : 2 * j + 1] = best
        stat[:RH, 2 * j + 1 : 2 * j + 2] = jnp.sum(expo, axis=1, keepdims=True)
        masked = logit + bias
        top = jnp.max(masked, axis=1, keepdims=True)
        stat[RH : RH + ROWS, 2 * j : 2 * j + 1] = top
        stat[RH : RH + ROWS, 2 * j + 1 : 2 * j + 2] = jnp.sum(
            jnp.exp2((masked - top) * log2e), axis=1, keepdims=True
        )
        keys_ref[j] = pieces[j][:, KPAD:]
    stat[:RH, 2 * count : 2 * count + 1] = coeff * weight
    stat[RH + ROWS :, :] = jnp.zeros((128 - ROWS, 128), f32)
    turned = jnp.transpose(stat[...])
    pairs = [(turned[2 * j : 2 * j + 1], turned[2 * j + 1 : 2 * j + 2]) for j in range(count)]
    best, total = merge([(prev_ref[0:1, :], prev_ref[1:2, :])] + pairs)
    rows = [best, total] + [p[0] for p in pairs]
    if len(rows) < 7:
        rows.append(jnp.zeros((7 - len(rows), STATS), f32))
    rows.append(turned[2 * count : 2 * count + 1])
    stat_ref[...] = jnp.concatenate(rows, axis=0)


def forward(bases, first, positions, prev, q_all, pieces):
    count = len(pieces)
    keys = PIECE * count
    vmem = pl.BlockSpec(memory_space=pltpu.VMEM)
    return pl.pallas_call(
        functools.partial(forward_kernel, count, first),
        in_specs=[pl.BlockSpec(memory_space=pltpu.SMEM)] + [vmem] * (3 + count),
        out_specs=[vmem] * 4,
        out_shape=[
            pltpu.VMEM((count, RH, PIECE), bf16),
            pltpu.VMEM((count, ROWS, PIECE), f32),
            pltpu.VMEM((count, PIECE, DI), bf16),
            pltpu.VMEM((8, STATS), f32),
        ],
        scratch_shapes=[pltpu.VMEM((STATS, 128), f32)],
        compiler_params=pltpu.CompilerParams(vmem_limit_bytes=VMEM_LIMIT),
        cost_estimate=pl.CostEstimate(
            flops=2 * RH * keys * 1536, bytes_accessed=2 * RH * keys, transcendentals=RH * keys
        ),
        name="forward",
    )(bases, positions, prev, q_all, *pieces)


def in_vmem(arrays):
    return [pltpu.with_memory_space_constraint(a, pltpu.VMEM) for a in arrays]


def backward_keys_kernel(sizes, *refs):
    n = len(sizes)
    place_ref, base_ref, pos_ref = refs[:3]
    stats = refs[3 : 6 + n]
    e_refs = refs[6 + n : 6 + 2 * n]
    logit_refs = refs[6 + 2 * n : 6 + 3 * n]
    key_refs = refs[6 + 3 * n : 6 + 4 * n]
    q_ref, dk_ref, grad_ref, factor = refs[6 + 4 * n :]
    flat = [(j, i) for j in range(n) for i in range(sizes[j])]
    other_refs = stats[:3]
    stat_refs = stats[3:]
    pairs = [(stat_refs[n - 1][0:1, :], stat_refs[n - 1][1:2, :])]
    for bits in (1, 2, 3):
        got = other_refs[bits - 1]
        pair = []
        for r in range(2):
            parts = [got[r : r + 1, (s ^ bits) * 384 : (s ^ bits) * 384 + 384] for s in range(4)]
            pair.append(jnp.concatenate(parts + [got[r : r + 1, RH:]], axis=1))
        pairs.append(tuple(pair))
    gbest, total = merge(pairs)
    inverse = 1.0 / total
    rows = [inverse, gbest]
    for j, i in flat:
        rows.append(
            jnp.exp2((stat_refs[j][2 + i : 3 + i, :] - gbest) * expo_scale)
            * (inverse * (1.0 / HEADS))
        )
    rows.append(jnp.zeros((128 - len(rows), STATS), f32))
    factor[...] = jnp.transpose(jnp.concatenate(rows, axis=0))
    top = factor[RH : RH + ROWS, 1:2]
    inverse = factor[RH : RH + ROWS, 0:1]
    repeat = (
        lax.broadcasted_iota(jnp.int32, (ROWS, BLOCK), 1) % ROWS
        == lax.broadcasted_iota(jnp.int32, (ROWS, BLOCK), 0)
    ).astype(bf16)
    weight_rows = stat_refs[0][7:8, :RH]
    at = 0
    for j in range(n):
        spreads = []
        for i in range(sizes[j]):
            k = at + i
            scaled = e_refs[j][i].astype(f32) * factor[:RH, 2 + k : 3 + k]
            target = jnp.sum(scaled.reshape(HEADS, ROWS, PIECE), axis=0)
            visible = key_positions(base_ref[k]) <= pos_ref[:, 0:1]
            masked = jnp.where(visible, logit_refs[j][i], negative)
            predicted = jnp.exp2((masked - top) * log2e) * inverse
            value = jnp.where(visible, loss_scale * (predicted - target), 0.0)
            rounded = value.astype(bf16)
            grad_ref[:, k * PIECE : (k + 1) * PIECE] = rounded.astype(f32)
            spreads.append(tn(rounded, repeat))
        spread = jnp.concatenate(spreads, axis=0)
        keys_mat = key_refs[j][...].reshape(sizes[j] * PIECE, DI)
        dk = None
        for r in range(RH // BLOCK):
            iq = q_ref[r * BLOCK : (r + 1) * BLOCK, KPAD:]
            inner = nt(keys_mat, iq)
            weight = weight_rows[:, r * BLOCK : (r + 1) * BLOCK]
            head_grads = jnp.where(inner > 0.0, spread * weight, 0.0).astype(bf16)
            term = nn(head_grads, iq)
            dk = term if dk is None else dk + term
        for i in range(sizes[j]):
            dk_ref[place_ref[at + i]] = dk[i * PIECE : (i + 1) * PIECE].astype(bf16)
        at += sizes[j]


def tn(left, right):
    return lax.dot_general(left, right, (((0,), (0,)), ((), ())), preferred_element_type=f32)


def head_grads_of(q_ref, keys_mat, grad):
    heads = BLOCK // ROWS
    keys = keys_mat.shape[0]
    inner = nt(q_ref[:, KPAD:], keys_mat)
    weight = coeff * weight_of(q_ref[:, :KPAD])
    spread = jnp.broadcast_to(grad[None], (heads, ROWS, keys)).reshape(BLOCK, keys)
    return jnp.where(inner > 0.0, weight * spread, 0.0).astype(bf16)


def backward_keys(place, bases, positions, others, stats, expos, logits, keys_list, q_all):
    sizes = tuple(e.shape[0] for e in expos)
    count = sum(sizes)
    keys = PIECE * count
    vmem = pl.BlockSpec(memory_space=pltpu.VMEM)
    smem = pl.BlockSpec(memory_space=pltpu.SMEM)
    held = in_vmem([*stats, *expos, *logits, *keys_list])
    return pl.pallas_call(
        functools.partial(backward_keys_kernel, sizes),
        in_specs=[smem, smem] + [vmem] * (5 + 4 * len(sizes)),
        out_specs=[vmem] * 2,
        scratch_shapes=[pltpu.VMEM((STATS, 128), f32)],
        out_shape=[
            jax.ShapeDtypeStruct((count, PIECE, DI), bf16),
            jax.ShapeDtypeStruct((ROWS, keys), f32),
        ],
        compiler_params=pltpu.CompilerParams(vmem_limit_bytes=VMEM_LIMIT),
        cost_estimate=pl.CostEstimate(
            flops=8 * RH * keys * 128, bytes_accessed=2 * RH * keys, transcendentals=0
        ),
        name="backward_keys",
    )(place, bases, positions, *others, *held, q_all)


def backward_queries_kernel(q_ref, grad_ref, *refs):
    key_refs, dq_ref, keys_ref = refs[:-2], refs[-2], refs[-1]

    @pl.when(pl.program_id(0) == 0)
    def _():
        at = 0
        for ref in key_refs:
            count = ref.shape[0]
            keys_ref[at : at + count * PIECE, :] = ref[...].reshape(count * PIECE, DI)
            at += count * PIECE

    dq = nn(head_grads_of(q_ref, keys_ref[...], grad_ref[...]), keys_ref[...])
    for j in range(BLOCK // ROWS):
        dq_ref[0, :, j * DI : (j + 1) * DI] = dq[j * ROWS : (j + 1) * ROWS].astype(bf16)


def backward_queries(q_all, keys_list, grad):
    keys = grad.shape[1]
    return pl.pallas_call(
        backward_queries_kernel,
        grid=(RH // BLOCK,),
        in_specs=[
            pl.BlockSpec((BLOCK, KPAD + DI), lambda i: (i, 0)),
            pl.BlockSpec((ROWS, keys), lambda i: (0, 0)),
        ]
        + [pl.BlockSpec(k.shape, lambda i: (0, 0, 0)) for k in keys_list],
        out_specs=pl.BlockSpec((1, ROWS, LOCAL * DI), lambda i: (i, 0, 0)),
        out_shape=jax.ShapeDtypeStruct((4, ROWS, LOCAL * DI), bf16),
        scratch_shapes=[pltpu.VMEM((keys, DI), bf16)],
        compiler_params=pltpu.CompilerParams(vmem_limit_bytes=VMEM_LIMIT),
        cost_estimate=pl.CostEstimate(
            flops=8 * RH * keys * 128, bytes_accessed=2 * RH * keys, transcendentals=0
        ),
        name="backward_queries",
    )(q_all, grad, *keys_list)


def flip(value, axis):
    return lax.ppermute(value, axis, [(0, 1), (1, 0)])


def head_xor(value, bits):
    return lax.ppermute(value, HEAD, [(i, i ^ bits) for i in range(4)])


def body(queries, kv_latent, index_queries, index_keys, head_weights, positions):
    z, yl, x = (lax.axis_index(a) for a in CTX)
    head = lax.axis_index(HEAD)
    with jax.named_scope("own_keys"):
        own_keys = jnp.concatenate(
            [
                jnp.transpose(lax.dynamic_slice_in_dim(kv_latent, head * 32, 32, 1)),
                jnp.zeros((32, KPAD - DL), bf16),
                lax.dynamic_slice_in_dim(index_keys, head * 32, 32, 0),
            ],
            axis=1,
        )
        own_keys = jnp.broadcast_to(own_keys[None], (8, 32, KPAD + DI))
        own_keys, queries, index_queries, head_weights = lax.optimization_barrier(
            (own_keys, queries, index_queries, head_weights)
        )
    with jax.named_scope("own_queries"):
        w = head_weights
        hi = lax.reduce_precision(w, 8, 7)
        mid = lax.reduce_precision(w - hi, 8, 7)
        low = w - hi - mid
        w_parts = jnp.stack([hi, mid, low] + [jnp.zeros_like(w)] * 5, axis=2).astype(bf16)
        q_own = jnp.concatenate([queries, index_queries, w_parts.reshape(ROWS, 128)], axis=1)
    with jax.named_scope("gather_queries"):
        q_yh = flip(q_own, "yh")
        q_core = flip(q_own, "core")
        q_both = flip(q_yh, "core")
        q_all = assemble([q_own, q_core, q_yh, q_both])

    def shift(value, s):
        return lax.ppermute(value, "x", [((i + s) % 4, i) for i in range(4)])

    with jax.named_scope("gather_keys"):
        p00 = lax.all_to_all(own_keys, "z", 0, 0, tiled=True).reshape(PIECE, KPAD + DI)
        p00, q_all = lax.optimization_barrier((p00, q_all))
        p01 = flip(p00, "yl")
        p10, p30 = shift(p00, 1), shift(p00, 3)
        p20 = shift(p00, 2)
        p11, p31 = shift(p01, 1), shift(p01, 3)
        p21 = flip(p20, "yl")
    groups = [
        [(0, 0, p00), (0, 1, p01)],
        [(1, 0, p10), (3, 0, p30), (2, 0, p20)],
        [(1, 1, p11), (3, 1, p31), (2, 1, p21)],
    ]
    flat = [entry for group in groups for entry in group]
    place = jnp.stack([((yl + b) % 2) * 4 + (x + s) % 4 for s, b, _ in flat])
    bases = place * 128 + head * 32
    pos = jnp.broadcast_to(positions[:, None], (ROWS, 128))
    stat = jnp.concatenate(
        [jnp.full((1, STATS), negative, f32), jnp.zeros((7, STATS), f32)], axis=0
    )
    expos, logits, stats, keys_list = [], [], [], []
    first = 0
    for group in groups:
        expo, logit, keys, stat = forward(
            bases, first, pos, stat, q_all, [p for _, _, p in group]
        )
        first += len(group)
        expos.append(expo)
        logits.append(logit)
        stats.append(stat)
        keys_list.append(keys)
    with jax.named_scope("exchange_stats"):
        others = [head_xor(stat, bits) for bits in (1, 2, 3)]
    dk, grad = backward_keys(
        place, bases, pos, others, stats, expos, logits, keys_list, q_all
    )
    dq = backward_queries(q_all, keys_list, grad)
    with jax.named_scope("reduce_keys"):
        dk_xy = lax.all_to_all(dk, ("yl", "x"), 0, 0, tiled=True)
        over_xy = dk_xy[0].astype(f32)
        for j in range(1, 8):
            over_xy = over_xy + dk_xy[j].astype(f32)
        dk_z = lax.all_to_all(over_xy.astype(bf16).reshape(8, 32, DI), "z", 0, 0, tiled=True)
        grad_keys = jnp.sum(dk_z.astype(f32), axis=0)
    with jax.named_scope("reduce_queries"):
        grad_queries = dq[0].astype(f32)
        for bits in (1, 2, 3):
            grad_queries = grad_queries + head_xor(dq[bits], bits).astype(f32)
    return (grad_queries, grad_keys)


def solution(mesh):
    fine = Mesh(mesh.devices.reshape(8, 2, 4, 2, 2), CTX + HEAD)
    in_specs = (
        P(CTX, HEAD),
        P(None, CTX),
        P(CTX, HEAD),
        P(CTX, None),
        P(CTX, HEAD),
        P(CTX),
    )
    out_specs = (P(CTX, HEAD), P(CTX + HEAD, None))
    return jax.shard_map(body, mesh=fine, in_specs=in_specs, out_specs=out_specs, check_vma=False)
```

```python
import functools
import math

import jax
import jax.numpy as jnp
from jax import lax
from jax.experimental import pallas as pl
from jax.experimental.pallas import tpu as pltpu
from jax.sharding import Mesh, PartitionSpec as P

DL = 576
HEADS = 64
IHEADS = 64
DI = 128
ROWS = 24
KPAD = 640
LOCAL = 16
RH = ROWS * HEADS
BLOCK = 384
KEYS = 2048
PIECE = 256
STATS = RH + 128
IQ_AT = LOCAL * DL
W_AT = IQ_AT + LOCAL * DI
RAW = W_AT + 128
HALF = PIECE // 2
PACKED = 1408
VMEM_LIMIT = 28 * 1024 * 1024

negative = -1e30
loss_scale = 64.0
score_scale = 1.0 / math.sqrt(192.0)
expo_scale = score_scale / math.log(2.0)
log2e = 1.0 / math.log(2.0)
coeff = 1.0 / math.sqrt(IHEADS * DI)

CTX = ("z", "yl", "x")
HEAD = ("yh", "core")
f32 = jnp.float32
bf16 = jnp.bfloat16


def nt(left, right):
    return lax.dot_general(left, right, (((1,), (1,)), ((), ())), preferred_element_type=f32)


def nn(left, right):
    return lax.dot_general(left, right, (((1,), (0,)), ((), ())), preferred_element_type=f32)


def weight_of(q_block, at=DL):
    parts = q_block[:, at : at + 3].astype(f32)
    return parts[:, 0:1] + parts[:, 1:2] + parts[:, 2:3]


def is_logit_row():
    return lax.broadcasted_iota(jnp.int32, (1, STATS), 1) >= RH


def scale_row():
    return jnp.where(is_logit_row(), log2e, expo_scale)


def merge(pairs):
    best = pairs[0][0]
    for other, _ in pairs[1:]:
        best = jnp.maximum(best, other)
    total = None
    for other, part in pairs:
        term = part * jnp.exp2((other - best) * scale_row())
        total = term if total is None else total + term
    return best, total


def assemble_kernel(*refs):
    raws, q_ref = refs[:4], refs[4]
    lane = lax.broadcasted_iota(jnp.int32, (ROWS, 128), 1)
    for b in range(4):
        weights = raws[b][:, W_AT : W_AT + 128].astype(f32)
        for pair in range(LOCAL // 2):
            rows = []
            for j in (2 * pair, 2 * pair + 1):
                start = j * DL - (j % 2) * 64
                wide = raws[b][:, start : start + KPAD].astype(f32)
                if j % 2:
                    wide = pltpu.roll(wide, KPAD - 64, 1)
                held = pltpu.roll(weights, (64 - 8 * j) % 128, 1)
                last = jnp.where(lane < 64, wide[:, 512:], jnp.where(lane < 67, held, 0.0))
                iq = raws[b][:, IQ_AT + j * DI : IQ_AT + (j + 1) * DI].astype(f32)
                rows.append(jnp.concatenate([wide[:, :512], last, iq], axis=1))
            at = (b * LOCAL + 2 * pair) * ROWS
            q_ref[at : at + 2 * ROWS, :] = jnp.concatenate(rows, axis=0).astype(bf16)


def assemble(raws):
    return pl.pallas_call(
        assemble_kernel,
        grid=(1,),
        in_specs=[pl.BlockSpec((ROWS, RAW), lambda i: (0, 0))] * 4,
        out_specs=pl.BlockSpec((RH, KPAD + DI), lambda i: (0, 0)),
        out_shape=jax.ShapeDtypeStruct((RH, KPAD + DI), bf16),
        compiler_params=pltpu.CompilerParams(vmem_limit_bytes=VMEM_LIMIT),
        cost_estimate=pl.CostEstimate(flops=0, bytes_accessed=5000000, transcendentals=0),
        name="assemble",
    )(*raws)


def key_positions(base):
    lane = lax.broadcasted_iota(jnp.int32, (1, PIECE), 1)
    return base + (lane % HALF // 16) * 1024 + lane % 16 + lane // HALF * 16


def unpack(piece):
    tails = piece[:, 1024:1152].astype(f32)
    keep = lax.broadcasted_iota(jnp.int32, (HALF, 128), 1) < KPAD - DL
    first = jnp.where(keep, tails, 0.0).astype(bf16)
    second = jnp.where(keep, pltpu.roll(tails, 64, 1), 0.0).astype(bf16)
    latents = jnp.concatenate(
        [
            jnp.concatenate([piece[:, :512], first], axis=1),
            jnp.concatenate([piece[:, 512:1024], second], axis=1),
        ],
        axis=0,
    )
    return latents, jnp.concatenate([piece[:, 1152:1280], piece[:, 1280:]], axis=0)


def forward_kernel(count, first, *refs):
    base_ref, pos_ref, prev_ref, q_ref = refs[:4]
    pieces = refs[4 : 4 + count]
    e_ref, logit_ref, keys_ref, own_ref, total_ref, stat = refs[4 + count :]
    weight = weight_of(q_ref[:, :KPAD])

    def products(j):
        latents, index_part = unpack(pieces[j][...])
        keys_ref[j] = index_part
        part = nt(q_ref[:, :KPAD], latents)
        inner = nt(q_ref[:, KPAD:], index_part)
        weighted = jnp.maximum(inner, 0.0) * weight
        return part, coeff * jnp.sum(weighted.reshape(HEADS, ROWS, PIECE), axis=0)

    ready = products(0)
    for j in range(count):
        part, logit = ready
        if j + 1 < count:
            ready = products(j + 1)
        kpos = key_positions(base_ref[first + j])
        bias = jnp.where(kpos <= pos_ref[:, 0:1], 0.0, negative)
        part = (part.reshape(HEADS, ROWS, PIECE) + bias[None]).reshape(RH, PIECE)
        best = jnp.max(part, axis=1, keepdims=True)
        logit_ref[j] = logit
        expo = jnp.exp2((part - best) * expo_scale)
        e_ref[j] = expo.astype(bf16)
        stat[:RH, 2 * j : 2 * j + 1] = best
        stat[:RH, 2 * j + 1 : 2 * j + 2] = jnp.sum(expo, axis=1, keepdims=True)
        masked = logit + bias
        top = jnp.max(masked, axis=1, keepdims=True)
        stat[RH : RH + ROWS, 2 * j : 2 * j + 1] = top
        stat[RH : RH + ROWS, 2 * j + 1 : 2 * j + 2] = jnp.sum(
            jnp.exp2((masked - top) * log2e), axis=1, keepdims=True
        )
    stat[:RH, 2 * count : 2 * count + 1] = coeff * weight
    stat[RH + ROWS :, :] = jnp.zeros((128 - ROWS, 128), f32)
    turned = jnp.transpose(stat[...])
    pairs = [(turned[2 * j : 2 * j + 1], turned[2 * j + 1 : 2 * j + 2]) for j in range(count)]
    best, total = merge([(prev_ref[0:1, :], prev_ref[1:2, :])] + pairs)
    total_ref[...] = jnp.concatenate([best, total], axis=0)
    rows = [turned[2 * count : 2 * count + 1]] + [p[0] for p in pairs]
    rows.append(jnp.zeros((8 - len(rows), STATS), f32))
    own_ref[...] = jnp.concatenate(rows, axis=0)


def forward(bases, first, positions, prev, q_all, pieces):
    count = len(pieces)
    keys = PIECE * count
    vmem = pl.BlockSpec(memory_space=pltpu.VMEM)
    return pl.pallas_call(
        functools.partial(forward_kernel, count, first),
        in_specs=[pl.BlockSpec(memory_space=pltpu.SMEM)] + [vmem] * (3 + count),
        out_specs=[vmem] * 5,
        out_shape=[
            pltpu.VMEM((count, RH, PIECE), bf16),
            pltpu.VMEM((count, ROWS, PIECE), f32),
            pltpu.VMEM((count, PIECE, DI), bf16),
            pltpu.VMEM((8, STATS), f32),
            pltpu.VMEM((2, STATS), f32),
        ],
        scratch_shapes=[pltpu.VMEM((STATS, 128), f32)],
        compiler_params=pltpu.CompilerParams(vmem_limit_bytes=VMEM_LIMIT),
        cost_estimate=pl.CostEstimate(
            flops=2 * RH * keys * 1536, bytes_accessed=2 * RH * keys, transcendentals=RH * keys
        ),
        name="forward",
    )(bases, positions, prev, q_all, *pieces)


def in_vmem(arrays):
    return [pltpu.with_memory_space_constraint(a, pltpu.VMEM) for a in arrays]


def backward_keys_kernel(sizes, *refs):
    n = len(sizes)
    place_ref, base_ref, pos_ref = refs[:3]
    total_refs = refs[3:7]
    stat_refs = refs[7 : 7 + n]
    e_refs = refs[7 + n : 7 + 2 * n]
    logit_refs = refs[7 + 2 * n : 7 + 3 * n]
    key_refs = refs[7 + 3 * n : 7 + 4 * n]
    q_ref, dk_ref, grad_ref, factor = refs[7 + 4 * n :]
    flat = [(j, i) for j in range(n) for i in range(sizes[j])]
    pairs = [(total_refs[0][0:1, :], total_refs[0][1:2, :])]
    for bits in (1, 2, 3):
        got = total_refs[bits]
        pair = []
        for r in range(2):
            parts = [got[r : r + 1, (s ^ bits) * 384 : (s ^ bits) * 384 + 384] for s in range(4)]
            pair.append(jnp.concatenate(parts + [got[r : r + 1, RH:]], axis=1))
        pairs.append(tuple(pair))
    gbest, total = merge(pairs)
    inverse = 1.0 / total
    rows = [inverse, gbest]
    for j, i in flat:
        rows.append(
            jnp.exp2((stat_refs[j][1 + i : 2 + i, :] - gbest) * expo_scale)
            * (inverse * (1.0 / HEADS))
        )
    rows.append(jnp.zeros((128 - len(rows), STATS), f32))
    factor[...] = jnp.transpose(jnp.concatenate(rows, axis=0))
    top = factor[RH : RH + ROWS, 1:2]
    inverse = factor[RH : RH + ROWS, 0:1]
    repeat = (
        lax.broadcasted_iota(jnp.int32, (ROWS, BLOCK), 1) % ROWS
        == lax.broadcasted_iota(jnp.int32, (ROWS, BLOCK), 0)
    ).astype(bf16)
    weight_rows = stat_refs[0][0:1, :RH]
    at = 0
    for j in range(n):
        spreads = []
        for i in range(sizes[j]):
            k = at + i
            scaled = e_refs[j][i].astype(f32) * factor[:RH, 2 + k : 3 + k]
            target = jnp.sum(scaled.reshape(HEADS, ROWS, PIECE), axis=0)
            visible = key_positions(base_ref[k]) <= pos_ref[:, 0:1]
            masked = jnp.where(visible, logit_refs[j][i], negative)
            predicted = jnp.exp2((masked - top) * log2e) * inverse
            value = jnp.where(visible, loss_scale * (predicted - target), 0.0)
            rounded = value.astype(bf16)
            grad_ref[:, k * PIECE : (k + 1) * PIECE] = rounded.astype(f32)
            spreads.append(tn(rounded, repeat))
        spread = jnp.concatenate(spreads, axis=0)
        keys_mat = key_refs[j][...].reshape(sizes[j] * PIECE, DI)
        dk = None
        for r in range(RH // BLOCK):
            iq = q_ref[r * BLOCK : (r + 1) * BLOCK, KPAD:]
            inner = nt(keys_mat, iq)
            weight = weight_rows[:, r * BLOCK : (r + 1) * BLOCK]
            head_grads = jnp.where(inner > 0.0, spread * weight, 0.0).astype(bf16)
            term = nn(head_grads, iq)
            dk = term if dk is None else dk + term
        for i in range(sizes[j]):
            dk_ref[place_ref[at + i]] = dk[i * PIECE : (i + 1) * PIECE].astype(bf16)
        at += sizes[j]


def tn(left, right):
    return lax.dot_general(left, right, (((0,), (0,)), ((), ())), preferred_element_type=f32)


def head_grads_of(q_ref, keys_mat, grad):
    heads = BLOCK // ROWS
    keys = keys_mat.shape[0]
    inner = nt(q_ref[:, KPAD:], keys_mat)
    weight = coeff * weight_of(q_ref[:, :KPAD])
    spread = jnp.broadcast_to(grad[None], (heads, ROWS, keys)).reshape(BLOCK, keys)
    return jnp.where(inner > 0.0, weight * spread, 0.0).astype(bf16)


def backward_keys(place, bases, positions, others, stats, expos, logits, keys_list, q_all):
    sizes = tuple(e.shape[0] for e in expos)
    count = sum(sizes)
    keys = PIECE * count
    vmem = pl.BlockSpec(memory_space=pltpu.VMEM)
    smem = pl.BlockSpec(memory_space=pltpu.SMEM)
    held = in_vmem([*stats, *expos, *logits, *keys_list])
    return pl.pallas_call(
        functools.partial(backward_keys_kernel, sizes),
        in_specs=[smem, smem] + [vmem] * (6 + 4 * len(sizes)),
        out_specs=[vmem] * 2,
        scratch_shapes=[pltpu.VMEM((STATS, 128), f32)],
        out_shape=[
            jax.ShapeDtypeStruct((count, PIECE, DI), bf16),
            jax.ShapeDtypeStruct((ROWS, keys), f32),
        ],
        compiler_params=pltpu.CompilerParams(vmem_limit_bytes=VMEM_LIMIT),
        cost_estimate=pl.CostEstimate(
            flops=8 * RH * keys * 128, bytes_accessed=2 * RH * keys, transcendentals=0
        ),
        name="backward_keys",
    )(place, bases, positions, *others, *held, q_all)


def backward_queries_kernel(q_ref, grad_ref, *refs):
    key_refs, dq_ref, keys_ref = refs[:-2], refs[-2], refs[-1]

    @pl.when(pl.program_id(0) == 0)
    def _():
        at = 0
        for ref in key_refs:
            count = ref.shape[0]
            keys_ref[at : at + count * PIECE, :] = ref[...].reshape(count * PIECE, DI)
            at += count * PIECE

    dq = nn(head_grads_of(q_ref, keys_ref[...], grad_ref[...]), keys_ref[...])
    for j in range(BLOCK // ROWS):
        dq_ref[0, :, j * DI : (j + 1) * DI] = dq[j * ROWS : (j + 1) * ROWS].astype(bf16)


def backward_queries(q_all, keys_list, grad):
    keys = grad.shape[1]
    return pl.pallas_call(
        backward_queries_kernel,
        grid=(RH // BLOCK,),
        in_specs=[
            pl.BlockSpec((BLOCK, KPAD + DI), lambda i: (i, 0)),
            pl.BlockSpec((ROWS, keys), lambda i: (0, 0)),
        ]
        + [pl.BlockSpec(k.shape, lambda i: (0, 0, 0)) for k in keys_list],
        out_specs=pl.BlockSpec((1, ROWS, LOCAL * DI), lambda i: (i, 0, 0)),
        out_shape=jax.ShapeDtypeStruct((4, ROWS, LOCAL * DI), bf16),
        scratch_shapes=[pltpu.VMEM((keys, DI), bf16)],
        compiler_params=pltpu.CompilerParams(vmem_limit_bytes=VMEM_LIMIT),
        cost_estimate=pl.CostEstimate(
            flops=8 * RH * keys * 128, bytes_accessed=2 * RH * keys, transcendentals=0
        ),
        name="backward_queries",
    )(q_all, grad, *keys_list)


def flip(value, axis):
    return lax.ppermute(value, axis, [(0, 1), (1, 0)])


def head_xor(value, bits):
    return lax.ppermute(value, HEAD, [(i, i ^ bits) for i in range(4)])


def body(queries, kv_latent, index_queries, index_keys, head_weights, positions):
    z, yl, x = (lax.axis_index(a) for a in CTX)
    head = lax.axis_index(HEAD)
    with jax.named_scope("own_keys"):
        kv = jnp.transpose(lax.dynamic_slice_in_dim(kv_latent, head * 32, 32, 1))
        ik = lax.dynamic_slice_in_dim(index_keys, head * 32, 32, 0)
        own_keys = jnp.concatenate(
            [kv[:16, :512], kv[16:, :512], kv[:16, 512:], kv[16:, 512:], ik[:16], ik[16:]], axis=1
        )
        own_keys = jnp.broadcast_to(own_keys[None], (8, 16, PACKED))
        own_keys, queries, index_queries, head_weights = lax.optimization_barrier(
            (own_keys, queries, index_queries, head_weights)
        )
    with jax.named_scope("own_queries"):
        w = head_weights
        hi = lax.reduce_precision(w, 8, 7)
        mid = lax.reduce_precision(w - hi, 8, 7)
        low = w - hi - mid
        w_parts = jnp.stack([hi, mid, low] + [jnp.zeros_like(w)] * 5, axis=2).astype(bf16)
        q_own = jnp.concatenate([queries, index_queries, w_parts.reshape(ROWS, 128)], axis=1)
    with jax.named_scope("gather_queries"):
        q_yh = flip(q_own, "yh")
        q_core = flip(q_own, "core")
        q_both = flip(q_yh, "core")
        q_all = assemble([q_own, q_core, q_yh, q_both])

    def shift(value, s):
        return lax.ppermute(value, "x", [((i + s) % 4, i) for i in range(4)])

    with jax.named_scope("gather_keys"):
        p00 = lax.all_to_all(own_keys, "z", 0, 0, tiled=True).reshape(HALF, PACKED)
        p00, q_all = lax.optimization_barrier((p00, q_all))
        p01 = flip(p00, "yl")
        p10, p30 = shift(p00, 1), shift(p00, 3)
        p20 = shift(p00, 2)
        p11, p31 = shift(p01, 1), shift(p01, 3)
        p21 = flip(p20, "yl")
    groups = [
        [(0, 0, p00), (0, 1, p01)],
        [(1, 0, p10), (3, 0, p30), (2, 0, p20)],
        [(1, 1, p11), (3, 1, p31), (2, 1, p21)],
    ]
    flat = [entry for group in groups for entry in group]
    place = jnp.stack([((yl + b) % 2) * 4 + (x + s) % 4 for s, b, _ in flat])
    bases = place * 128 + head * 32
    pos = jnp.broadcast_to(positions[:, None], (ROWS, 128))
    stat = jnp.concatenate(
        [jnp.full((1, STATS), negative, f32), jnp.zeros((1, STATS), f32)], axis=0
    )
    expos, logits, stats, keys_list = [], [], [], []
    first = 0
    for group in groups:
        expo, logit, keys, own, stat = forward(
            bases, first, pos, stat, q_all, [p for _, _, p in group]
        )
        first += len(group)
        expos.append(expo)
        logits.append(logit)
        stats.append(own)
        keys_list.append(keys)
    with jax.named_scope("exchange_stats"):
        others = [head_xor(stat, bits) for bits in (1, 2, 3)]
    dk, grad = backward_keys(
        place, bases, pos, [stat] + others, stats, expos, logits, keys_list, q_all
    )
    dq = backward_queries(q_all, keys_list, grad)
    with jax.named_scope("reduce_keys"):
        dk_xy = lax.all_to_all(dk, ("yl", "x"), 0, 0, tiled=True)
        over_xy = dk_xy[0].astype(f32)
        for j in range(1, 8):
            over_xy = over_xy + dk_xy[j].astype(f32)
        over_xy = over_xy.astype(bf16).reshape(2, 8, 16, DI)
        dk_z = lax.all_to_all(
            jnp.transpose(over_xy, (1, 0, 2, 3)).reshape(8, 32, DI), "z", 0, 0, tiled=True
        )
        grad_keys = jnp.sum(dk_z.astype(f32), axis=0)
    with jax.named_scope("reduce_queries"):
        grad_queries = dq[0].astype(f32)
        for bits in (1, 2, 3):
            grad_queries = grad_queries + head_xor(dq[bits], bits).astype(f32)
    return (grad_queries, grad_keys)


def solution(mesh):
    fine = Mesh(mesh.devices.reshape(8, 2, 4, 2, 2), CTX + HEAD)
    in_specs = (
        P(CTX, HEAD),
        P(None, CTX),
        P(CTX, HEAD),
        P(CTX, None),
        P(CTX, HEAD),
        P(CTX),
    )
    out_specs = (P(CTX, HEAD), P(CTX + HEAD, None))
    return jax.shard_map(body, mesh=fine, in_specs=in_specs, out_specs=out_specs, check_vma=False)
```

```python
import functools
import math

import jax
import jax.numpy as jnp
from jax import lax
from jax.experimental import pallas as pl
from jax.experimental.pallas import tpu as pltpu
from jax.sharding import Mesh, PartitionSpec as P

DL = 576
HEADS = 64
IHEADS = 64
DI = 128
ROWS = 24
KPAD = 640
LOCAL = 16
RH = ROWS * HEADS
BLOCK = 384
KEYS = 2048
PIECE = 256
STATS = RH + 128
IQ_AT = LOCAL * DL
W_AT = IQ_AT + LOCAL * DI
RAW = W_AT + 128
HALF = PIECE // 2
PACKED = 1408
VMEM_LIMIT = 28 * 1024 * 1024

negative = -1e30
loss_scale = 64.0
score_scale = 1.0 / math.sqrt(192.0)
expo_scale = score_scale / math.log(2.0)
log2e = 1.0 / math.log(2.0)
coeff = 1.0 / math.sqrt(IHEADS * DI)

CTX = ("z", "yl", "x")
HEAD = ("yh", "core")
f32 = jnp.float32
bf16 = jnp.bfloat16


def nt(left, right):
    return lax.dot_general(left, right, (((1,), (1,)), ((), ())), preferred_element_type=f32)


def nn(left, right):
    return lax.dot_general(left, right, (((1,), (0,)), ((), ())), preferred_element_type=f32)


def weight_of(q_block, at=DL):
    parts = q_block[:, at : at + 3].astype(f32)
    return parts[:, 0:1] + parts[:, 1:2] + parts[:, 2:3]


def is_logit_row():
    return lax.broadcasted_iota(jnp.int32, (1, STATS), 1) >= RH


def scale_row():
    return jnp.where(is_logit_row(), log2e, expo_scale)


def merge(pairs):
    best = pairs[0][0]
    for other, _ in pairs[1:]:
        best = jnp.maximum(best, other)
    total = None
    for other, part in pairs:
        term = part * jnp.exp2((other - best) * scale_row())
        total = term if total is None else total + term
    return best, total


def assemble_kernel(*refs):
    raws, q_ref = refs[:4], refs[4]
    lane = lax.broadcasted_iota(jnp.int32, (ROWS, 128), 1)
    for b in range(4):
        weights = raws[b][:, W_AT : W_AT + 128].astype(f32)
        for pair in range(LOCAL // 2):
            rows = []
            for j in (2 * pair, 2 * pair + 1):
                start = j * DL - (j % 2) * 64
                wide = raws[b][:, start : start + KPAD].astype(f32)
                if j % 2:
                    wide = pltpu.roll(wide, KPAD - 64, 1)
                held = pltpu.roll(weights, (64 - 8 * j) % 128, 1)
                last = jnp.where(lane < 64, wide[:, 512:], jnp.where(lane < 67, held, 0.0))
                iq = raws[b][:, IQ_AT + j * DI : IQ_AT + (j + 1) * DI].astype(f32)
                rows.append(jnp.concatenate([wide[:, :512], last, iq], axis=1))
            at = (b * LOCAL + 2 * pair) * ROWS
            q_ref[at : at + 2 * ROWS, :] = jnp.concatenate(rows, axis=0).astype(bf16)


def assemble(raws):
    return pl.pallas_call(
        assemble_kernel,
        grid=(1,),
        in_specs=[pl.BlockSpec((ROWS, RAW), lambda i: (0, 0))] * 4,
        out_specs=pl.BlockSpec((RH, KPAD + DI), lambda i: (0, 0)),
        out_shape=jax.ShapeDtypeStruct((RH, KPAD + DI), bf16),
        compiler_params=pltpu.CompilerParams(vmem_limit_bytes=VMEM_LIMIT),
        cost_estimate=pl.CostEstimate(flops=0, bytes_accessed=50000000, transcendentals=0),
        name="assemble",
    )(*raws)


def key_positions(base):
    lane = lax.broadcasted_iota(jnp.int32, (1, PIECE), 1)
    return base + (lane % HALF // 16) * 1024 + lane % 16 + lane // HALF * 16


def unpack(piece):
    tails = piece[:, 1024:1152].astype(f32)
    keep = lax.broadcasted_iota(jnp.int32, (HALF, 128), 1) < KPAD - DL
    first = jnp.where(keep, tails, 0.0).astype(bf16)
    second = jnp.where(keep, pltpu.roll(tails, 64, 1), 0.0).astype(bf16)
    latents = jnp.concatenate(
        [
            jnp.concatenate([piece[:, :512], first], axis=1),
            jnp.concatenate([piece[:, 512:1024], second], axis=1),
        ],
        axis=0,
    )
    return latents, jnp.concatenate([piece[:, 1152:1280], piece[:, 1280:]], axis=0)


def forward_kernel(count, first, *refs):
    base_ref, pos_ref, prev_ref, q_ref = refs[:4]
    pieces = refs[4 : 4 + count]
    e_ref, logit_ref, keys_ref, own_ref, total_ref, stat = refs[4 + count :]
    weight = weight_of(q_ref[:, :KPAD])

    def products(j):
        latents, index_part = unpack(pieces[j][...])
        keys_ref[j] = index_part
        part = nt(q_ref[:, :KPAD], latents)
        inner = nt(q_ref[:, KPAD:], index_part)
        weighted = jnp.maximum(inner, 0.0) * weight
        return part, coeff * jnp.sum(weighted.reshape(HEADS, ROWS, PIECE), axis=0)

    ready = products(0)
    for j in range(count):
        part, logit = ready
        if j + 1 < count:
            ready = products(j + 1)
        kpos = key_positions(base_ref[first + j])
        bias = jnp.where(kpos <= pos_ref[:, 0:1], 0.0, negative)
        part = (part.reshape(HEADS, ROWS, PIECE) + bias[None]).reshape(RH, PIECE)
        best = jnp.max(part, axis=1, keepdims=True)
        logit_ref[j] = logit
        expo = jnp.exp2((part - best) * expo_scale)
        e_ref[j] = expo.astype(bf16)
        stat[:RH, 2 * j : 2 * j + 1] = best
        stat[:RH, 2 * j + 1 : 2 * j + 2] = jnp.sum(expo, axis=1, keepdims=True)
        masked = logit + bias
        top = jnp.max(masked, axis=1, keepdims=True)
        stat[RH : RH + ROWS, 2 * j : 2 * j + 1] = top
        stat[RH : RH + ROWS, 2 * j + 1 : 2 * j + 2] = jnp.sum(
            jnp.exp2((masked - top) * log2e), axis=1, keepdims=True
        )
    stat[:RH, 2 * count : 2 * count + 1] = coeff * weight
    stat[RH + ROWS :, :] = jnp.zeros((128 - ROWS, 128), f32)
    turned = jnp.transpose(stat[...])
    pairs = [(turned[2 * j : 2 * j + 1], turned[2 * j + 1 : 2 * j + 2]) for j in range(count)]
    best, total = merge([(prev_ref[0:1, :], prev_ref[1:2, :])] + pairs)
    total_ref[...] = jnp.concatenate([best, total], axis=0)
    rows = [turned[2 * count : 2 * count + 1]] + [p[0] for p in pairs]
    rows.append(jnp.zeros((8 - len(rows), STATS), f32))
    own_ref[...] = jnp.concatenate(rows, axis=0)


def forward(bases, first, positions, prev, q_all, pieces):
    count = len(pieces)
    keys = PIECE * count
    vmem = pl.BlockSpec(memory_space=pltpu.VMEM)
    return pl.pallas_call(
        functools.partial(forward_kernel, count, first),
        in_specs=[pl.BlockSpec(memory_space=pltpu.SMEM)] + [vmem] * (3 + count),
        out_specs=[vmem] * 5,
        out_shape=[
            pltpu.VMEM((count, RH, PIECE), bf16),
            pltpu.VMEM((count, ROWS, PIECE), f32),
            pltpu.VMEM((count, PIECE, DI), bf16),
            pltpu.VMEM((8, STATS), f32),
            pltpu.VMEM((2, STATS), f32),
        ],
        scratch_shapes=[pltpu.VMEM((STATS, 128), f32)],
        compiler_params=pltpu.CompilerParams(vmem_limit_bytes=VMEM_LIMIT),
        cost_estimate=pl.CostEstimate(
            flops=2 * RH * keys * 1536, bytes_accessed=2 * RH * keys, transcendentals=RH * keys
        ),
        name="forward",
    )(bases, positions, prev, q_all, *pieces)


def in_vmem(arrays):
    return [pltpu.with_memory_space_constraint(a, pltpu.VMEM) for a in arrays]


def backward_keys_kernel(sizes, *refs):
    n = len(sizes)
    place_ref, base_ref, pos_ref = refs[:3]
    total_refs = refs[3:7]
    stat_refs = refs[7 : 7 + n]
    e_refs = refs[7 + n : 7 + 2 * n]
    logit_refs = refs[7 + 2 * n : 7 + 3 * n]
    key_refs = refs[7 + 3 * n : 7 + 4 * n]
    q_ref, dk_ref, grad_ref, factor = refs[7 + 4 * n :]
    flat = [(j, i) for j in range(n) for i in range(sizes[j])]
    pairs = [(total_refs[0][0:1, :], total_refs[0][1:2, :])]
    for bits in (1, 2, 3):
        got = total_refs[bits]
        pair = []
        for r in range(2):
            parts = [got[r : r + 1, (s ^ bits) * 384 : (s ^ bits) * 384 + 384] for s in range(4)]
            pair.append(jnp.concatenate(parts + [got[r : r + 1, RH:]], axis=1))
        pairs.append(tuple(pair))
    gbest, total = merge(pairs)
    inverse = 1.0 / total
    rows = [inverse, gbest]
    for j, i in flat:
        rows.append(
            jnp.exp2((stat_refs[j][1 + i : 2 + i, :] - gbest) * expo_scale)
            * (inverse * (1.0 / HEADS))
        )
    rows.append(jnp.zeros((128 - len(rows), STATS), f32))
    factor[...] = jnp.transpose(jnp.concatenate(rows, axis=0))
    top = factor[RH : RH + ROWS, 1:2]
    inverse = factor[RH : RH + ROWS, 0:1]
    repeat = (
        lax.broadcasted_iota(jnp.int32, (ROWS, BLOCK), 1) % ROWS
        == lax.broadcasted_iota(jnp.int32, (ROWS, BLOCK), 0)
    ).astype(bf16)
    weight_rows = stat_refs[0][0:1, :RH]
    at = 0
    for j in range(n):
        spreads = []
        for i in range(sizes[j]):
            k = at + i
            scaled = e_refs[j][i].astype(f32) * factor[:RH, 2 + k : 3 + k]
            target = jnp.sum(scaled.reshape(HEADS, ROWS, PIECE), axis=0)
            visible = key_positions(base_ref[k]) <= pos_ref[:, 0:1]
            masked = jnp.where(visible, logit_refs[j][i], negative)
            predicted = jnp.exp2((masked - top) * log2e) * inverse
            value = jnp.where(visible, loss_scale * (predicted - target), 0.0)
            rounded = value.astype(bf16)
            grad_ref[:, k * PIECE : (k + 1) * PIECE] = rounded.astype(f32)
            spreads.append(tn(rounded, repeat))
        spread = jnp.concatenate(spreads, axis=0)
        keys_mat = key_refs[j][...].reshape(sizes[j] * PIECE, DI)
        dk = None
        for r in range(RH // BLOCK):
            iq = q_ref[r * BLOCK : (r + 1) * BLOCK, KPAD:]
            inner = nt(keys_mat, iq)
            weight = weight_rows[:, r * BLOCK : (r + 1) * BLOCK]
            head_grads = jnp.where(inner > 0.0, spread * weight, 0.0).astype(bf16)
            term = nn(head_grads, iq)
            dk = term if dk is None else dk + term
        for i in range(sizes[j]):
            dk_ref[place_ref[at + i]] = dk[i * PIECE : (i + 1) * PIECE].astype(bf16)
        at += sizes[j]


def tn(left, right):
    return lax.dot_general(left, right, (((0,), (0,)), ((), ())), preferred_element_type=f32)


def head_grads_of(q_ref, keys_mat, grad):
    heads = BLOCK // ROWS
    keys = keys_mat.shape[0]
    inner = nt(q_ref[:, KPAD:], keys_mat)
    weight = coeff * weight_of(q_ref[:, :KPAD])
    spread = jnp.broadcast_to(grad[None], (heads, ROWS, keys)).reshape(BLOCK, keys)
    return jnp.where(inner > 0.0, weight * spread, 0.0).astype(bf16)


def backward_keys(place, bases, positions, others, stats, expos, logits, keys_list, q_all):
    sizes = tuple(e.shape[0] for e in expos)
    count = sum(sizes)
    keys = PIECE * count
    vmem = pl.BlockSpec(memory_space=pltpu.VMEM)
    smem = pl.BlockSpec(memory_space=pltpu.SMEM)
    held = in_vmem([*stats, *expos, *logits, *keys_list])
    return pl.pallas_call(
        functools.partial(backward_keys_kernel, sizes),
        in_specs=[smem, smem] + [vmem] * (6 + 4 * len(sizes)),
        out_specs=[vmem] * 2,
        scratch_shapes=[pltpu.VMEM((STATS, 128), f32)],
        out_shape=[
            jax.ShapeDtypeStruct((count, PIECE, DI), bf16),
            pltpu.VMEM((ROWS, keys), f32),
        ],
        compiler_params=pltpu.CompilerParams(vmem_limit_bytes=VMEM_LIMIT),
        cost_estimate=pl.CostEstimate(
            flops=8 * RH * keys * 128, bytes_accessed=2 * RH * keys, transcendentals=0
        ),
        name="backward_keys",
    )(place, bases, positions, *others, *held, q_all)


def backward_queries_kernel(q_ref, grad_ref, *refs):
    key_refs, dq_ref = refs[:-1], refs[-1]
    keys_mat = jnp.concatenate([r[...].reshape(r.shape[0] * PIECE, DI) for r in key_refs], axis=0)
    for r in range(RH // BLOCK):
        q_block = q_ref.at[r * BLOCK : (r + 1) * BLOCK]
        dq = nn(head_grads_of(q_block, keys_mat, grad_ref[...]), keys_mat)
        for j in range(BLOCK // ROWS):
            dq_ref[r, :, j * DI : (j + 1) * DI] = dq[j * ROWS : (j + 1) * ROWS].astype(bf16)


def backward_queries(q_all, keys_list, grad):
    vmem = pl.BlockSpec(memory_space=pltpu.VMEM)
    return pl.pallas_call(
        backward_queries_kernel,
        in_specs=[vmem] * (2 + len(keys_list)),
        out_specs=vmem,
        out_shape=jax.ShapeDtypeStruct((4, ROWS, LOCAL * DI), bf16),
        compiler_params=pltpu.CompilerParams(vmem_limit_bytes=VMEM_LIMIT),
        cost_estimate=pl.CostEstimate(
            flops=32 * RH * KEYS * 128, bytes_accessed=2 * RH * KEYS, transcendentals=0
        ),
        name="backward_queries",
    )(q_all, *in_vmem([grad, *keys_list]))


def flip(value, axis):
    return lax.ppermute(value, axis, [(0, 1), (1, 0)])


def head_xor(value, bits):
    return lax.ppermute(value, HEAD, [(i, i ^ bits) for i in range(4)])


def body(queries, kv_latent, index_queries, index_keys, head_weights, positions):
    z, yl, x = (lax.axis_index(a) for a in CTX)
    head = lax.axis_index(HEAD)
    with jax.named_scope("own_keys"):
        kv = jnp.transpose(lax.dynamic_slice_in_dim(kv_latent, head * 32, 32, 1))
        ik = lax.dynamic_slice_in_dim(index_keys, head * 32, 32, 0)
        own_keys = jnp.concatenate(
            [kv[:16, :512], kv[16:, :512], kv[:16, 512:], kv[16:, 512:], ik[:16], ik[16:]], axis=1
        )
        own_keys = jnp.broadcast_to(own_keys[None], (8, 16, PACKED))
        own_keys, queries, index_queries, head_weights = lax.optimization_barrier(
            (own_keys, queries, index_queries, head_weights)
        )
    with jax.named_scope("own_queries"):
        w = head_weights
        hi = lax.reduce_precision(w, 8, 7)
        mid = lax.reduce_precision(w - hi, 8, 7)
        low = w - hi - mid
        w_parts = jnp.stack([hi, mid, low] + [jnp.zeros_like(w)] * 5, axis=2).astype(bf16)
        q_own = jnp.concatenate([queries, index_queries, w_parts.reshape(ROWS, 128)], axis=1)
    with jax.named_scope("gather_queries"):
        q_yh = flip(q_own, "yh")
        q_core = flip(q_own, "core")
        q_both = flip(q_yh, "core")
        q_all = assemble([q_own, q_core, q_yh, q_both])

    def shift(value, s):
        return lax.ppermute(value, "x", [((i + s) % 4, i) for i in range(4)])

    with jax.named_scope("gather_keys"):
        p00 = lax.all_to_all(own_keys, "z", 0, 0, tiled=True).reshape(HALF, PACKED)
        p01 = flip(p00, "yl")
        p20 = shift(p00, 2)
        later, q_all = lax.optimization_barrier((p00, q_all))
        p10, p30 = shift(later, 1), shift(later, 3)
        p11, p31 = shift(p01, 1), shift(p01, 3)
        p21 = flip(p20, "yl")
    groups = [
        [(0, 0, p00), (0, 1, p01)],
        [(1, 0, p10), (3, 0, p30), (2, 0, p20)],
        [(1, 1, p11), (3, 1, p31), (2, 1, p21)],
    ]
    flat = [entry for group in groups for entry in group]
    place = jnp.stack([((yl + b) % 2) * 4 + (x + s) % 4 for s, b, _ in flat])
    bases = place * 128 + head * 32
    pos = jnp.broadcast_to(positions[:, None], (ROWS, 128))
    stat = jnp.concatenate(
        [jnp.full((1, STATS), negative, f32), jnp.zeros((1, STATS), f32)], axis=0
    )
    expos, logits, stats, keys_list = [], [], [], []
    first = 0
    for group in groups:
        expo, logit, keys, own, stat = forward(
            bases, first, pos, stat, q_all, [p for _, _, p in group]
        )
        first += len(group)
        expos.append(expo)
        logits.append(logit)
        stats.append(own)
        keys_list.append(keys)
    with jax.named_scope("exchange_stats"):
        others = [head_xor(stat, bits) for bits in (1, 2, 3)]
    dk, grad = backward_keys(
        place, bases, pos, [stat] + others, stats, expos, logits, keys_list, q_all
    )
    dq = backward_queries(q_all, keys_list, grad)
    with jax.named_scope("reduce_keys"):
        dk_xy = lax.all_to_all(dk, ("yl", "x"), 0, 0, tiled=True)
        over_xy = dk_xy[0].astype(f32)
        for j in range(1, 8):
            over_xy = over_xy + dk_xy[j].astype(f32)
        over_xy = over_xy.astype(bf16).reshape(2, 8, 16, DI)
        dk_z = lax.all_to_all(
            jnp.transpose(over_xy, (1, 0, 2, 3)).reshape(8, 32, DI), "z", 0, 0, tiled=True
        )
        grad_keys = jnp.sum(dk_z.astype(f32), axis=0)
    with jax.named_scope("reduce_queries"):
        grad_queries = dq[0].astype(f32)
        for bits in (1, 2, 3):
            grad_queries = grad_queries + head_xor(dq[bits], bits).astype(f32)
    return (grad_queries, grad_keys)


def solution(mesh):
    fine = Mesh(mesh.devices.reshape(8, 2, 4, 2, 2), CTX + HEAD)
    in_specs = (
        P(CTX, HEAD),
        P(None, CTX),
        P(CTX, HEAD),
        P(CTX, None),
        P(CTX, HEAD),
        P(CTX),
    )
    out_specs = (P(CTX, HEAD), P(CTX + HEAD, None))
    return jax.shard_map(body, mesh=fine, in_specs=in_specs, out_specs=out_specs, check_vma=False)
```

```python
import functools
import math

import jax
import jax.numpy as jnp
from jax import lax
from jax.experimental import pallas as pl
from jax.experimental.pallas import tpu as pltpu
from jax.sharding import Mesh, PartitionSpec as P

DL = 576
HEADS = 64
IHEADS = 64
DI = 128
ROWS = 24
KPAD = 640
LOCAL = 16
RH = ROWS * HEADS
BLOCK = 384
KEYS = 2048
PIECE = 256
STATS = RH + 128
IQ_AT = LOCAL * DL
W_AT = IQ_AT + LOCAL * DI
RAW = W_AT + 128
HALF = PIECE // 2
PACKED = 1408
VMEM_LIMIT = 28 * 1024 * 1024

negative = -1e30
loss_scale = 64.0
score_scale = 1.0 / math.sqrt(192.0)
expo_scale = score_scale / math.log(2.0)
log2e = 1.0 / math.log(2.0)
coeff = 1.0 / math.sqrt(IHEADS * DI)

CTX = ("z", "yl", "x")
HEAD = ("yh", "core")
f32 = jnp.float32
bf16 = jnp.bfloat16


def nt(left, right):
    return lax.dot_general(left, right, (((1,), (1,)), ((), ())), preferred_element_type=f32)


def nn(left, right):
    return lax.dot_general(left, right, (((1,), (0,)), ((), ())), preferred_element_type=f32)


def weight_of(q_block, at=DL):
    parts = q_block[:, at : at + 3].astype(f32)
    return parts[:, 0:1] + parts[:, 1:2] + parts[:, 2:3]


def is_logit_row():
    return lax.broadcasted_iota(jnp.int32, (1, STATS), 1) >= RH


def scale_row():
    return jnp.where(is_logit_row(), log2e, expo_scale)


def merge(pairs):
    best = pairs[0][0]
    for other, _ in pairs[1:]:
        best = jnp.maximum(best, other)
    total = None
    for other, part in pairs:
        term = part * jnp.exp2((other - best) * scale_row())
        total = term if total is None else total + term
    return best, total


def assemble_kernel(*refs):
    raws, q_ref = refs[:4], refs[4]
    lane = lax.broadcasted_iota(jnp.int32, (ROWS, 128), 1)
    for b in range(4):
        weights = raws[b][:, W_AT : W_AT + 128].astype(f32)
        for pair in range(LOCAL // 2):
            rows = []
            for j in (2 * pair, 2 * pair + 1):
                start = j * DL - (j % 2) * 64
                wide = raws[b][:, start : start + KPAD].astype(f32)
                if j % 2:
                    wide = pltpu.roll(wide, KPAD - 64, 1)
                held = pltpu.roll(weights, (64 - 8 * j) % 128, 1)
                last = jnp.where(lane < 64, wide[:, 512:], jnp.where(lane < 67, held, 0.0))
                iq = raws[b][:, IQ_AT + j * DI : IQ_AT + (j + 1) * DI].astype(f32)
                rows.append(jnp.concatenate([wide[:, :512], last, iq], axis=1))
            at = (b * LOCAL + 2 * pair) * ROWS
            q_ref[at : at + 2 * ROWS, :] = jnp.concatenate(rows, axis=0).astype(bf16)


def assemble(raws):
    return pl.pallas_call(
        assemble_kernel,
        grid=(1,),
        in_specs=[pl.BlockSpec((ROWS, RAW), lambda i: (0, 0))] * 4,
        out_specs=pl.BlockSpec((RH, KPAD + DI), lambda i: (0, 0)),
        out_shape=jax.ShapeDtypeStruct((RH, KPAD + DI), bf16),
        compiler_params=pltpu.CompilerParams(vmem_limit_bytes=VMEM_LIMIT),
        cost_estimate=pl.CostEstimate(flops=0, bytes_accessed=50000000, transcendentals=0),
        name="assemble",
    )(*raws)


def key_positions(base):
    lane = lax.broadcasted_iota(jnp.int32, (1, PIECE), 1)
    return base + (lane % HALF // 16) * 1024 + lane % 16 + lane // HALF * 16


def unpack(piece):
    tails = piece[:, 1024:1152].astype(f32)
    keep = lax.broadcasted_iota(jnp.int32, (HALF, 128), 1) < KPAD - DL
    first = jnp.where(keep, tails, 0.0).astype(bf16)
    second = jnp.where(keep, pltpu.roll(tails, 64, 1), 0.0).astype(bf16)
    latents = jnp.concatenate(
        [
            jnp.concatenate([piece[:, :512], first], axis=1),
            jnp.concatenate([piece[:, 512:1024], second], axis=1),
        ],
        axis=0,
    )
    return latents, jnp.concatenate([piece[:, 1152:1280], piece[:, 1280:]], axis=0)


def forward_kernel(count, first, *refs):
    base_ref, pos_ref, prev_ref, q_ref = refs[:4]
    pieces = refs[4 : 4 + count]
    e_ref, logit_ref, keys_ref, own_ref, total_ref, stat = refs[4 + count :]
    weight = weight_of(q_ref[:, :KPAD])

    def products(j):
        latents, index_part = unpack(pieces[j][...])
        keys_ref[j] = index_part
        part = nt(q_ref[:, :KPAD], latents)
        inner = nt(q_ref[:, KPAD:], index_part)
        weighted = jnp.maximum(inner, 0.0) * weight
        return part, coeff * jnp.sum(weighted.reshape(HEADS, ROWS, PIECE), axis=0)

    ready = products(0)
    for j in range(count):
        part, logit = ready
        if j + 1 < count:
            ready = products(j + 1)
        kpos = key_positions(base_ref[first + j])
        bias = jnp.where(kpos <= pos_ref[:, 0:1], 0.0, negative)
        part = (part.reshape(HEADS, ROWS, PIECE) + bias[None]).reshape(RH, PIECE)
        best = jnp.max(part, axis=1, keepdims=True)
        logit_ref[j] = logit
        expo = jnp.exp2((part - best) * expo_scale)
        e_ref[j] = expo.astype(bf16)
        stat[:RH, 2 * j : 2 * j + 1] = best
        stat[:RH, 2 * j + 1 : 2 * j + 2] = jnp.sum(expo, axis=1, keepdims=True)
        masked = logit + bias
        top = jnp.max(masked, axis=1, keepdims=True)
        stat[RH : RH + ROWS, 2 * j : 2 * j + 1] = top
        stat[RH : RH + ROWS, 2 * j + 1 : 2 * j + 2] = jnp.sum(
            jnp.exp2((masked - top) * log2e), axis=1, keepdims=True
        )
    stat[:RH, 2 * count : 2 * count + 1] = coeff * weight
    stat[RH + ROWS :, :] = jnp.zeros((128 - ROWS, 128), f32)
    turned = jnp.transpose(stat[...])
    pairs = [(turned[2 * j : 2 * j + 1], turned[2 * j + 1 : 2 * j + 2]) for j in range(count)]
    best, total = merge([(prev_ref[0:1, :], prev_ref[1:2, :])] + pairs)
    total_ref[...] = jnp.concatenate([best, total], axis=0)
    rows = [turned[2 * count : 2 * count + 1]] + [p[0] for p in pairs]
    rows.append(jnp.zeros((8 - len(rows), STATS), f32))
    own_ref[...] = jnp.concatenate(rows, axis=0)


def forward(bases, first, positions, prev, q_all, pieces):
    count = len(pieces)
    keys = PIECE * count
    vmem = pl.BlockSpec(memory_space=pltpu.VMEM)
    return pl.pallas_call(
        functools.partial(forward_kernel, count, first),
        in_specs=[pl.BlockSpec(memory_space=pltpu.SMEM)] + [vmem] * (3 + count),
        out_specs=[vmem] * 5,
        out_shape=[
            pltpu.VMEM((count, RH, PIECE), bf16),
            pltpu.VMEM((count, ROWS, PIECE), f32),
            pltpu.VMEM((count, PIECE, DI), bf16),
            pltpu.VMEM((8, STATS), f32),
            pltpu.VMEM((2, STATS), f32),
        ],
        scratch_shapes=[pltpu.VMEM((STATS, 128), f32)],
        compiler_params=pltpu.CompilerParams(vmem_limit_bytes=VMEM_LIMIT),
        cost_estimate=pl.CostEstimate(
            flops=2 * RH * keys * 1536, bytes_accessed=2 * RH * keys, transcendentals=RH * keys
        ),
        name="forward",
    )(bases, positions, prev, q_all, *pieces)


def in_vmem(arrays):
    return [pltpu.with_memory_space_constraint(a, pltpu.VMEM) for a in arrays]


def backward_keys_kernel(sizes, *refs):
    n = len(sizes)
    place_ref, base_ref, pos_ref = refs[:3]
    total_refs = refs[3:7]
    stat_refs = refs[7 : 7 + n]
    e_refs = refs[7 + n : 7 + 2 * n]
    logit_refs = refs[7 + 2 * n : 7 + 3 * n]
    key_refs = refs[7 + 3 * n : 7 + 4 * n]
    q_ref, dk_ref, grad_ref, factor = refs[7 + 4 * n :]
    flat = [(j, i) for j in range(n) for i in range(sizes[j])]
    pairs = [(total_refs[0][0:1, :], total_refs[0][1:2, :])]
    for bits in (1, 2, 3):
        got = total_refs[bits]
        pair = []
        for r in range(2):
            parts = [got[r : r + 1, (s ^ bits) * 384 : (s ^ bits) * 384 + 384] for s in range(4)]
            pair.append(jnp.concatenate(parts + [got[r : r + 1, RH:]], axis=1))
        pairs.append(tuple(pair))
    gbest, total = merge(pairs)
    inverse = 1.0 / total
    rows = [inverse, gbest]
    for j, i in flat:
        rows.append(
            jnp.exp2((stat_refs[j][1 + i : 2 + i, :] - gbest) * expo_scale)
            * (inverse * (1.0 / HEADS))
        )
    rows.append(jnp.zeros((128 - len(rows), STATS), f32))
    factor[...] = jnp.transpose(jnp.concatenate(rows, axis=0))
    top = factor[RH : RH + ROWS, 1:2]
    inverse = factor[RH : RH + ROWS, 0:1]
    repeat = (
        lax.broadcasted_iota(jnp.int32, (ROWS, BLOCK), 1) % ROWS
        == lax.broadcasted_iota(jnp.int32, (ROWS, BLOCK), 0)
    ).astype(bf16)
    weight_rows = stat_refs[0][0:1, :RH]
    at = 0
    for j in range(n):
        spreads = []
        for i in range(sizes[j]):
            k = at + i
            scaled = e_refs[j][i].astype(f32) * factor[:RH, 2 + k : 3 + k]
            target = jnp.sum(scaled.reshape(HEADS, ROWS, PIECE), axis=0)
            visible = key_positions(base_ref[k]) <= pos_ref[:, 0:1]
            masked = jnp.where(visible, logit_refs[j][i], negative)
            predicted = jnp.exp2((masked - top) * log2e) * inverse
            value = jnp.where(visible, loss_scale * (predicted - target), 0.0)
            rounded = value.astype(bf16)
            grad_ref[:, k * PIECE : (k + 1) * PIECE] = rounded.astype(f32)
            spreads.append(tn(rounded, repeat))
        spread = jnp.concatenate(spreads, axis=0)
        keys_mat = key_refs[j][...].reshape(sizes[j] * PIECE, DI)
        dk = None
        for r in range(RH // BLOCK):
            iq = q_ref[r * BLOCK : (r + 1) * BLOCK, KPAD:]
            inner = nt(keys_mat, iq)
            weight = weight_rows[:, r * BLOCK : (r + 1) * BLOCK]
            head_grads = jnp.where(inner > 0.0, spread * weight, 0.0).astype(bf16)
            term = nn(head_grads, iq)
            dk = term if dk is None else dk + term
        for i in range(sizes[j]):
            dk_ref[place_ref[at + i]] = dk[i * PIECE : (i + 1) * PIECE].astype(bf16)
        at += sizes[j]


def tn(left, right):
    return lax.dot_general(left, right, (((0,), (0,)), ((), ())), preferred_element_type=f32)


def head_grads_of(q_ref, keys_mat, grad):
    heads = BLOCK // ROWS
    keys = keys_mat.shape[0]
    inner = nt(q_ref[:, KPAD:], keys_mat)
    weight = coeff * weight_of(q_ref[:, :KPAD])
    spread = jnp.broadcast_to(grad[None], (heads, ROWS, keys)).reshape(BLOCK, keys)
    return jnp.where(inner > 0.0, weight * spread, 0.0).astype(bf16)


def backward_keys(place, bases, positions, others, stats, expos, logits, keys_list, q_all):
    sizes = tuple(e.shape[0] for e in expos)
    count = sum(sizes)
    keys = PIECE * count
    vmem = pl.BlockSpec(memory_space=pltpu.VMEM)
    smem = pl.BlockSpec(memory_space=pltpu.SMEM)
    held = in_vmem([*stats, *expos, *logits, *keys_list])
    return pl.pallas_call(
        functools.partial(backward_keys_kernel, sizes),
        in_specs=[smem, smem] + [vmem] * (6 + 4 * len(sizes)),
        out_specs=[vmem] * 2,
        scratch_shapes=[pltpu.VMEM((STATS, 128), f32)],
        out_shape=[
            jax.ShapeDtypeStruct((count, PIECE, DI), bf16),
            pltpu.VMEM((ROWS, keys), f32),
        ],
        compiler_params=pltpu.CompilerParams(vmem_limit_bytes=VMEM_LIMIT),
        cost_estimate=pl.CostEstimate(
            flops=8 * RH * keys * 128, bytes_accessed=2 * RH * keys, transcendentals=0
        ),
        name="backward_keys",
    )(place, bases, positions, *others, *held, q_all)


def backward_queries_kernel(q_ref, grad_ref, *refs):
    key_refs, dq_ref = refs[:-1], refs[-1]
    keys_mat = jnp.concatenate([r[...].reshape(r.shape[0] * PIECE, DI) for r in key_refs], axis=0)
    for r in range(RH // BLOCK):
        q_block = q_ref.at[r * BLOCK : (r + 1) * BLOCK]
        dq = nn(head_grads_of(q_block, keys_mat, grad_ref[...]), keys_mat)
        for j in range(BLOCK // ROWS):
            dq_ref[r, :, j * DI : (j + 1) * DI] = dq[j * ROWS : (j + 1) * ROWS].astype(bf16)


def backward_queries(q_all, keys_list, grad):
    vmem = pl.BlockSpec(memory_space=pltpu.VMEM)
    return pl.pallas_call(
        backward_queries_kernel,
        in_specs=[vmem] * (2 + len(keys_list)),
        out_specs=vmem,
        out_shape=jax.ShapeDtypeStruct((4, ROWS, LOCAL * DI), bf16),
        compiler_params=pltpu.CompilerParams(vmem_limit_bytes=VMEM_LIMIT),
        cost_estimate=pl.CostEstimate(
            flops=32 * RH * KEYS * 128, bytes_accessed=2 * RH * KEYS, transcendentals=0
        ),
        name="backward_queries",
    )(q_all, *in_vmem([grad, *keys_list]))


def flip(value, axis):
    return lax.ppermute(value, axis, [(0, 1), (1, 0)])


def head_xor(value, bits):
    return lax.ppermute(value, HEAD, [(i, i ^ bits) for i in range(4)])


def body(queries, kv_latent, index_queries, index_keys, head_weights, positions):
    z, yl, x = (lax.axis_index(a) for a in CTX)
    head = lax.axis_index(HEAD)
    with jax.named_scope("own_keys"):
        kv = jnp.transpose(lax.dynamic_slice_in_dim(kv_latent, head * 32, 32, 1))
        ik = lax.dynamic_slice_in_dim(index_keys, head * 32, 32, 0)
        own_keys = jnp.concatenate(
            [kv[:16, :512], kv[16:, :512], kv[:16, 512:], kv[16:, 512:], ik[:16], ik[16:]], axis=1
        )
        own_keys = jnp.broadcast_to(own_keys[None], (8, 16, PACKED))
        own_keys, queries, index_queries, head_weights = lax.optimization_barrier(
            (own_keys, queries, index_queries, head_weights)
        )
    with jax.named_scope("own_queries"):
        w = head_weights
        hi = lax.reduce_precision(w, 8, 7)
        mid = lax.reduce_precision(w - hi, 8, 7)
        low = w - hi - mid
        w_parts = jnp.stack([hi, mid, low] + [jnp.zeros_like(w)] * 5, axis=2).astype(bf16)
        q_own = jnp.concatenate([queries, index_queries, w_parts.reshape(ROWS, 128)], axis=1)
    with jax.named_scope("gather_queries"):
        q_yh = flip(q_own, "yh")
        q_core = flip(q_own, "core")
        q_both = flip(q_yh, "core")
        q_all = assemble([q_own, q_core, q_yh, q_both])

    def shift(value, s):
        return lax.ppermute(value, "x", [((i + s) % 4, i) for i in range(4)])

    with jax.named_scope("gather_keys"):
        p00 = lax.all_to_all(own_keys, "z", 0, 0, tiled=True).reshape(HALF, PACKED)
        p01 = flip(p00, "yl")
        p20 = shift(p00, 2)
        later, q_all = lax.optimization_barrier((p00, q_all))
        p10, p30 = shift(later, 1), shift(later, 3)
        p11, p31 = shift(p01, 1), shift(p01, 3)
        p21 = flip(p20, "yl")
    groups = [
        [(0, 0, p00), (0, 1, p01), (2, 0, p20)],
        [(1, 0, p10), (3, 0, p30)],
        [(1, 1, p11), (3, 1, p31), (2, 1, p21)],
    ]
    flat = [entry for group in groups for entry in group]
    place = jnp.stack([((yl + b) % 2) * 4 + (x + s) % 4 for s, b, _ in flat])
    bases = place * 128 + head * 32
    pos = jnp.broadcast_to(positions[:, None], (ROWS, 128))
    stat = jnp.concatenate(
        [jnp.full((1, STATS), negative, f32), jnp.zeros((1, STATS), f32)], axis=0
    )
    expos, logits, stats, keys_list = [], [], [], []
    first = 0
    for group in groups:
        expo, logit, keys, own, stat = forward(
            bases, first, pos, stat, q_all, [p for _, _, p in group]
        )
        first += len(group)
        expos.append(expo)
        logits.append(logit)
        stats.append(own)
        keys_list.append(keys)
    with jax.named_scope("exchange_stats"):
        others = [head_xor(stat, bits) for bits in (1, 2, 3)]
    dk, grad = backward_keys(
        place, bases, pos, [stat] + others, stats, expos, logits, keys_list, q_all
    )
    dq = backward_queries(q_all, keys_list, grad)
    with jax.named_scope("reduce_keys"):
        dk_xy = lax.all_to_all(dk, ("yl", "x"), 0, 0, tiled=True)
        over_xy = dk_xy[0].astype(f32)
        for j in range(1, 8):
            over_xy = over_xy + dk_xy[j].astype(f32)
        over_xy = over_xy.astype(bf16).reshape(2, 8, 16, DI)
        dk_z = lax.all_to_all(
            jnp.transpose(over_xy, (1, 0, 2, 3)).reshape(8, 32, DI), "z", 0, 0, tiled=True
        )
        grad_keys = jnp.sum(dk_z.astype(f32), axis=0)
    with jax.named_scope("reduce_queries"):
        grad_queries = dq[0].astype(f32)
        for bits in (1, 2, 3):
            grad_queries = grad_queries + head_xor(dq[bits], bits).astype(f32)
    return (grad_queries, grad_keys)


def solution(mesh):
    fine = Mesh(mesh.devices.reshape(8, 2, 4, 2, 2), CTX + HEAD)
    in_specs = (
        P(CTX, HEAD),
        P(None, CTX),
        P(CTX, HEAD),
        P(CTX, None),
        P(CTX, HEAD),
        P(CTX),
    )
    out_specs = (P(CTX, HEAD), P(CTX + HEAD, None))
    return jax.shard_map(body, mesh=fine, in_specs=in_specs, out_specs=out_specs, check_vma=False)
```
